32 devices in a mesh: face: 16 (over z, y, core), sub: 2 (over x).
Axes of the slice: x: 2, y: 2, z: 4, core: 2. Of those that a mesh axis runs over, the one named last changes fastest.
Arguments:
- nodes: bfloat16 [40960, 256], P(('face', 'sub')), may hold values from -6 to 6
- edges: bfloat16 [40960, 12, 256], P(('face', 'sub')), may hold values from -6 to 6
- neighbours: int32 [40960, 12], P(('face', 'sub')), may hold values from 0 to 1791
- valid: int32 [40960, 12], P(('face', 'sub')), may hold values 0 or 1
- send_lists: int32 [32, 2, 256], P(('face', 'sub')), may hold values from 0 to 1279
- edge_first: bfloat16 [768, 256], replicated, may hold values from -0.21875 to 0.21875
- edge_first_bias: bfloat16 [256], replicated, may hold values from -3 to 3
- edge_second: bfloat16 [256, 256], replicated, may hold values from -0.375 to 0.375
- edge_second_bias: bfloat16 [256], replicated, may hold values from -3 to 3
- edge_gain: bfloat16 [256], replicated, may hold values from 0.5 to 1.5
- edge_shift: bfloat16 [256], replicated, may hold values from -3 to 3
- node_first: bfloat16 [512, 256], replicated, may hold values from -0.25 to 0.25
- node_first_bias: bfloat16 [256], replicated, may hold values from -3 to 3
- node_second: bfloat16 [256, 256], replicated, may hold values from -0.375 to 0.375
- node_second_bias: bfloat16 [256], replicated, may hold values from -3 to 3
- node_gain: bfloat16 [256], replicated, may hold values from 0.5 to 1.5
- node_shift: bfloat16 [256], replicated, may hold values from -3 to 3
- cotangent: bfloat16 [40960, 256], P(('face', 'sub')), may hold values from -6 to 6
Outputs:
- mixed: bfloat16 [40960, 256], P(('face', 'sub'))
- grad_nodes: float32 [40960, 256], P(('face', 'sub'))
- grad_edges: bfloat16 [40960, 12, 256], P(('face', 'sub'))
- grad_edge_first: float32 [768, 256], replicated
- grad_edge_first_bias: float32 [256], replicated
- grad_edge_second: float32 [256, 256], replicated
- grad_edge_second_bias: float32 [256], replicated
- grad_edge_gain: float32 [256], replicated
- grad_edge_shift: float32 [256], replicated
- grad_node_first: float32 [512, 256], replicated
- grad_node_first_bias: float32 [256], replicated
- grad_node_second: float32 [256, 256], replicated
- grad_node_second_bias: float32 [256], replicated
- grad_node_gain: float32 [256], replicated
- grad_node_shift: float32 [256], replicated
The draws below stay inside these ranges and needn't reach their ends.
All inputs are finite; a program needn't handle non-finite values. No bound on the sum of `valid` on one device may be relied on, other than what follows from the above.
Results may differ from the reference program's by a relative error of at most 0.0084.
Values may be sent and summed in bfloat16 or wider, within the bound.
No kernel may reach another device: no remote copies, remote signals or barrier semaphores. Data moves between devices by JAX's collectives and lax.ppermute only.
A program may use at most 192 MiB of HBM per device.

```python
import jax
import jax.numpy as jnp
from jax import lax

LAT = 256
DEG = 12
NODE_DEV = 1280
HALO = 256
NODES = 40960
N_FACE = 16
N_SUB = 2


def set_ends(entries, rng, least, high):
    place = [jax.random.randint(jax.random.fold_in(rng, axis), (), 0, length) for axis, length in enumerate(entries.shape)]
    longest = entries.shape.index(max(entries.shape))
    neighbour = place[:longest] + [(place[longest] + 1) % entries.shape[longest]] + place[longest + 1:]
    return entries.at[tuple(place)].set(least).at[tuple(neighbour)].set(high)


def block_levels(own_key, dims, pieces, least, high):
    def one(dim, blocks):
        steps = jax.random.uniform(jax.random.fold_in(jax.random.fold_in(own_key, 6), dim), (blocks,), jnp.float32, least / len(pieces), high / len(pieces))
        return jnp.repeat(jnp.exp(steps), dims[dim] // blocks).reshape((-1,) + (1,) * (len(dims) - dim - 1))

    level = one(*pieces[0])
    for cut in pieces[1:]:
        level = level * one(*cut)
    return level


def noise(key, extent, scale, limit, shards=(), kind=jnp.bfloat16):
    array = jax.random.normal(key, extent, jnp.float32) * scale
    if len(shards) > 0:
        array = block_levels(key, extent, shards, -0.22, 0.18) * array
    return jnp.clip(array, min=-limit, max=limit).astype(kind)


def setup_inputs(seed: int = 0) -> dict:
    streams_of = jax.random.split(jax.random.key(seed), 19)
    return {
        "nodes": noise(streams_of[0], (NODES, LAT), 1.0, 6.0, ((0, 32),)),
        "edges": noise(streams_of[1], (NODES, DEG, LAT), 1.0, 6.0, ((0, 32),)),
        "neighbours": set_ends(jax.random.randint(streams_of[2], (NODES, DEG), 0, NODE_DEV + 2 * HALO), jax.random.fold_in(streams_of[2], 1), 0, (NODE_DEV + 2 * HALO) - 1).astype(jnp.int32),
        "valid": set_ends((jax.random.randint(streams_of[3], (NODES, DEG), 0, 4) < 3).astype(jnp.int32), jax.random.fold_in(streams_of[3], 1), 0, 1),
        "send_lists": set_ends(jax.random.randint(streams_of[4], (N_FACE * N_SUB, 2, HALO), 0, NODE_DEV), jax.random.fold_in(streams_of[4], 1), 0, NODE_DEV - 1).astype(jnp.int32),
        "edge_first": noise(streams_of[5], (3 * LAT, LAT), (3 * LAT) ** -0.5, 0.21875),
        "edge_first_bias": noise(streams_of[6], (LAT,), 0.5, 3.0),
        "edge_second": noise(streams_of[7], (LAT, LAT), LAT ** -0.5, 0.375),
        "edge_second_bias": noise(streams_of[8], (LAT,), 0.5, 3.0),
        "edge_gain": jnp.clip(jax.random.uniform(streams_of[9], (LAT,), jnp.float32, 0.5, 1.5), 0.5, 1.5).astype(jnp.bfloat16),
        "edge_shift": noise(streams_of[10], (LAT,), 0.5, 3.0),
        "node_first": noise(streams_of[11], (2 * LAT, LAT), (2 * LAT) ** -0.5, 0.25),
        "node_first_bias": noise(streams_of[12], (LAT,), 0.5, 3.0),
        "node_second": noise(streams_of[13], (LAT, LAT), LAT ** -0.5, 0.375),
        "node_second_bias": noise(streams_of[14], (LAT,), 0.5, 3.0),
        "node_gain": jnp.clip(jax.random.uniform(streams_of[15], (LAT,), jnp.float32, 0.5, 1.5), 0.5, 1.5).astype(jnp.bfloat16),
        "node_shift": noise(streams_of[16], (LAT,), 0.5, 3.0),
        "cotangent": noise(streams_of[17], (NODES, LAT), 1.0, 6.0, ((0, 32),)),
    }


@jax.custom_vjp
def low(v):
    return lax.optimization_barrier(v.astype(jnp.bfloat16)).astype(jnp.float32)

@jax.custom_vjp
def low_back(v):
    return v

def low_keep(v):
    return (low(v), None)

def low_pass(kept, grad):
    return (grad,)

def back_keep(v):
    return (v, None)

def back_low(kept, grad):
    return (low(grad),)
low.defvjp(low_keep, low_pass)
low_back.defvjp(back_keep, back_low)

def matmul(left, right):
    return jnp.dot(left, right, precision=lax.Precision.HIGHEST, preferred_element_type=jnp.float32)

def layer_norm(values, gain, shift):
    centre = values - lax.optimization_barrier(jnp.mean(values, axis=-1, keepdims=True))
    spread = lax.optimization_barrier(jnp.mean(centre * centre, axis=-1, keepdims=True))
    return centre * lax.rsqrt(spread + 1e-05) * gain + shift

def device_block(params, items):
    e_first, e_first_bias, e_second, e_second_bias, e_gain, e_shift, n_first, n_first_bias, n_second, n_second_bias, n_gain, n_shift = params
    own_rows, from_prev, from_next, edge_rows, neigh_rows, valid_rows = items
    table = jnp.concatenate([own_rows, from_prev, from_next], axis=0)
    senders = jnp.take(table, neigh_rows.reshape(-1).astype(jnp.int32), axis=0)
    receivers = jnp.repeat(own_rows, DEG, axis=0)
    joined = jnp.concatenate([receivers, senders, edge_rows.reshape(-1, LAT)], axis=1)
    pre_first = low_back(matmul(joined, e_first) + e_first_bias)
    act_first = low(jax.nn.silu(pre_first))
    pre_second = low_back(matmul(act_first, e_second) + e_second_bias)
    message = layer_norm(pre_second, e_gain, e_shift)
    weights = valid_rows.astype(jnp.float32).reshape(-1, 1)
    gathered = low(lax.optimization_barrier(jnp.sum((message * weights).reshape(-1, DEG, LAT), axis=1)))
    node_in = jnp.concatenate([own_rows, gathered], axis=1)
    pre_third = low_back(matmul(node_in, n_first) + n_first_bias)
    act_third = low(jax.nn.silu(pre_third))
    pre_fourth = low_back(matmul(act_third, n_second) + n_second_bias)
    return own_rows + layer_norm(pre_fourth, n_gain, n_shift)

def reference(nodes, edges, neighbours, valid, send_lists, edge_first, edge_first_bias, edge_second, edge_second_bias, edge_gain, edge_shift, node_first, node_first_bias, node_second, node_second_bias, node_gain, node_shift, cotangent):
    count = N_FACE * N_SUB
    params = tuple((w.astype(jnp.float32) for w in (edge_first, edge_first_bias, edge_second, edge_second_bias, edge_gain, edge_shift, node_first, node_first_bias, node_second, node_second_bias, node_gain, node_shift)))
    start_nodes = nodes.astype(jnp.float32)
    start_edges = edges.astype(jnp.float32)
    device_ids = jnp.arange(count, dtype=jnp.int32)
    face_ids = device_ids // N_SUB
    sub_ids = device_ids % N_SUB
    prev_ids = (face_ids - 1) % N_FACE * N_SUB + sub_ids
    next_ids = (face_ids + 1) % N_FACE * N_SUB + sub_ids
    neigh_all = neighbours.reshape(count, NODE_DEV, DEG)
    valid_all = valid.reshape(count, NODE_DEV, DEG)

    def forward(node_vals, edge_vals, weights):
        blocks = node_vals.reshape(count, NODE_DEV, LAT)
        to_next = jax.vmap(lambda rows, picks: jnp.take(rows, picks, axis=0))(blocks, send_lists[:, 0, :])
        to_prev = jax.vmap(lambda rows, picks: jnp.take(rows, picks, axis=0))(blocks, send_lists[:, 1, :])
        from_prev = low_back(jnp.take(to_next, prev_ids, axis=0))
        from_next = low_back(jnp.take(to_prev, next_ids, axis=0))
        edge_blocks = edge_vals.reshape(count, NODE_DEV, DEG, LAT)
        step = jax.checkpoint(lambda items: device_block(weights, items))
        result = lax.map(step, (blocks, from_prev, from_next, edge_blocks, neigh_all, valid_all))
        return result.reshape(-1, LAT)
    result, pull = jax.vjp(forward, start_nodes, start_edges, params)
    grad_x, grad_e, grad_w = pull(cotangent.astype(jnp.float32))
    return (result.astype(jnp.bfloat16), grad_x, grad_e.astype(jnp.bfloat16), grad_w[0], grad_w[1], grad_w[2], grad_w[3], grad_w[4], grad_w[5], grad_w[6], grad_w[7], grad_w[8], grad_w[9], grad_w[10], grad_w[11])
```

```python
import functools

import jax
import jax.numpy as jnp
from jax import lax
from jax.experimental import pallas as pl
from jax.experimental.pallas import tpu as pltpu
from jax.sharding import PartitionSpec as P

F32 = jnp.float32
BF16 = jnp.bfloat16
LANES = 128
BLOCK = 128
NODE_BLOCK = 256
BOTH = ("face", "sub")
VMEM_LIMIT = 60 * 1024 * 1024


def params(limit=VMEM_LIMIT):
    return pltpu.CompilerParams(vmem_limit_bytes=limit)


def cost(flops, moved):
    return pl.CostEstimate(flops=int(flops), bytes_accessed=int(moved), transcendentals=0)


def dot(left, right):
    return jnp.dot(left, right, preferred_element_type=F32)


def dot_rows(left, right):
    return lax.dot_general(left, right, (((0,), (0,)), ((), ())), preferred_element_type=F32)


def dot_back(left, right):
    return lax.dot_general(left, right, (((1,), (1,)), ((), ())), preferred_element_type=F32)


def down(row):
    return jnp.broadcast_to(row, (LANES, LANES)).T


def hot_lanes(index, first, count):
    lane = lax.broadcasted_iota(jnp.int32, (1, LANES), 1)
    tiles = [
        jnp.where(index == lane + (first + t * LANES), 1.0, 0.0).astype(BF16)
        for t in range(count // LANES)
    ]
    return jnp.concatenate(tiles, axis=1)


def hot_rows(index, first, count):
    row = lax.broadcasted_iota(jnp.int32, (count, 1), 0) + first
    return jnp.where(row == index, 1.0, 0.0).astype(BF16)


def row_mean(values):
    return jnp.mean(values, axis=-1, keepdims=True)


def col_sum(values):
    return jnp.sum(values, axis=0, keepdims=True)


def gate(values):
    sigma = 0.5 * jnp.tanh(0.5 * values) + 0.5
    act = values * sigma
    return act, sigma + act * (1.0 - sigma)


def norm(values):
    centre = values - row_mean(values)
    scale = lax.rsqrt(row_mean(centre * centre) + 1e-05)
    return centre * scale, scale


def pick_kernel(lists_ref, nodes_ref, next_ref, prev_ref):
    rows = nodes_ref.shape[0]
    halo = lists_ref.shape[1]
    for side, out_ref in ((0, next_ref), (1, prev_ref)):
        for at in range(0, halo, LANES):
            index = down(lists_ref[side : side + 1, at : at + LANES])
            out_ref[at : at + LANES, :] = dot(
                hot_lanes(index, 0, rows), nodes_ref[...]
            ).astype(BF16)


def pick(lists, nodes):
    halo, width = lists.shape[1], nodes.shape[1]
    out = jax.ShapeDtypeStruct((halo, width), BF16)
    return pl.pallas_call(
        pick_kernel,
        out_shape=(out, out),
        compiler_params=params(),
        cost_estimate=cost(4 * halo * nodes.size, 2 * nodes.size),
        name="pick_rows",
    )(lists, nodes)


def own_kernel(index_ref, nodes_ref, out_ref):
    rows = nodes_ref.shape[0]
    for k in range(index_ref.shape[0]):
        index = down(index_ref[k : k + 1, :])
        out_ref[k] = dot(hot_lanes(index, 0, rows), nodes_ref[...]).astype(BF16)


def own_senders(index, nodes):
    degree, rows = index.shape
    width = nodes.shape[1]
    return pl.pallas_call(
        own_kernel,
        grid=(rows // BLOCK,),
        in_specs=[
            pl.BlockSpec((degree, BLOCK), lambda i: (0, i)),
            pl.BlockSpec((rows, width), lambda i: (0, 0)),
        ],
        out_specs=pl.BlockSpec((degree, BLOCK, width), lambda i: (0, i, 0)),
        out_shape=jax.ShapeDtypeStruct((degree, rows, width), BF16),
        compiler_params=params(),
        cost_estimate=cost(2 * degree * rows * rows * width, 2 * degree * rows * width),
        name="own_senders",
    )(index, nodes)


def main_kernel(
    blocks,
    part_rows,
    place_ref,
    index_ref,
    valid_ref,
    edges_ref,
    own_ref,
    nodes_ref,
    halo_ref,
    cot_ref,
    vec_ref,
    w_first_ref,
    w_second_ref,
    n_first_ref,
    n_second_ref,
    mixed_ref,
    grad_nodes_ref,
    grad_a_ref,
    away_ref,
    keep_ref,
    snd_scr,
    act_scr,
    slope_scr,
    hat_scr,
    scale_scr,
    sum_scr,
    count_scr,
    up_scr,
    sec_scr,
    acc_scr,
):
    step = pl.program_id(0)
    degree = index_ref.shape[0]
    rows, width = nodes_ref.shape
    block = rows // blocks
    e_b1, e_b2, e_gain, e_shift, n_b1, n_b2, n_gain, n_shift = (
        vec_ref[i : i + 1, :] for i in range(8)
    )
    at_first, at_second = 0, 3 * width
    at_nfirst, at_nsecond, at_vec = 4 * width, 6 * width, 7 * width

    @pl.when(step < blocks)
    def forward():
        here = pl.ds(pl.multiple_of(step * block, block), block)
        joint = index_ref[...] * 2 + valid_ref[...]
        base = dot(nodes_ref[here, :], w_first_ref[:width, :]) + e_b1
        total = jnp.zeros((block, width), F32)
        count = jnp.zeros((block, LANES), F32)
        for k in range(degree):
            column = down(joint[k : k + 1, :])
            live = (column & 1).astype(F32)
            picked = dot(hot_lanes(column >> 1, rows, halo_ref.shape[0]), halo_ref[...])
            snd = (picked + own_ref[k].astype(F32)).astype(BF16)
            snd_scr[step, k] = snd
            joined = jnp.concatenate([snd, edges_ref[k]], axis=1)
            act, slope = gate(dot(joined, w_first_ref[width:, :]) + base)
            act = act.astype(BF16)
            act_scr[step, k] = act
            slope_scr[step, k] = slope.astype(BF16)
            hat, scale = norm(dot(act, w_second_ref[...]) + e_b2)
            hat_scr[step, k] = hat.astype(BF16)
            scale_scr[step, k] = scale * live
            total = total + hat * jnp.concatenate([live] * (width // LANES), axis=1)
            count = count + live
        sum_scr[here, :] = total
        count_scr[here, :] = count

    @pl.when(step == blocks)
    def node_stage():
        acc_scr[...] = jnp.zeros(acc_scr.shape, F32)

        @pl.loop(0, rows // NODE_BLOCK)
        def one_part(part):
            here = pl.ds(pl.multiple_of(part * NODE_BLOCK, NODE_BLOCK), NODE_BLOCK)
            x = nodes_ref[here, :]
            sums = sum_scr[here, :]
            counts = jnp.concatenate([count_scr[here, :]] * (width // LANES), axis=1)
            gathered = (sums * e_gain + counts * e_shift).astype(BF16)
            act, slope = gate(
                dot(jnp.concatenate([x, gathered], axis=1), n_first_ref[...]) + n_b1
            )
            act = act.astype(BF16)
            hat, scale = norm(dot(act, n_second_ref[...]) + n_b2)
            mixed_ref[here, :] = (x.astype(F32) + (hat * n_gain + n_shift)).astype(BF16)
            up = cot_ref[here, :].astype(F32)
            acc_scr[at_vec + 6 : at_vec + 7, :] += col_sum(up * hat)
            acc_scr[at_vec + 7 : at_vec + 8, :] += col_sum(up)
            scaled = up * n_gain
            grad_d = scale * (scaled - row_mean(scaled) - hat * row_mean(scaled * hat))
            grad_d = grad_d.astype(BF16)
            acc_scr[at_nsecond : at_nsecond + width, :] += dot_rows(act, grad_d)
            acc_scr[at_vec + 5 : at_vec + 6, :] += col_sum(grad_d.astype(F32))
            grad_c = (dot_back(grad_d, n_second_ref[...]) * slope).astype(BF16)
            acc_scr[at_nfirst : at_nfirst + width, :] += dot_rows(x, grad_c)
            acc_scr[at_nfirst + width : at_nfirst + 2 * width, :] += dot_rows(
                gathered, grad_c
            )
            acc_scr[at_vec + 4 : at_vec + 5, :] += col_sum(grad_c.astype(F32))
            grad_nodes_ref[here, :] = up + dot_back(grad_c, n_first_ref[:width, :])
            back = dot_back(grad_c, n_first_ref[width:, :])
            acc_scr[at_vec + 2 : at_vec + 3, :] += col_sum(back * sums)
            acc_scr[at_vec + 3 : at_vec + 4, :] += col_sum(back * counts)
            back = back * e_gain
            up_scr[here, :] = back - row_mean(back)

    @pl.when(step >= blocks)
    def backward():
        now = step - blocks
        here = pl.ds(pl.multiple_of(now * block, block), block)
        up = up_scr[here, :]
        total_a = jnp.zeros((block, width), F32)
        total_b = jnp.zeros((block, width), F32)
        for k in range(degree):
            hat = hat_scr[now, k].astype(F32)
            scale = jnp.concatenate([scale_scr[now, k]] * (width // LANES), axis=1)
            grad_b = (scale * (up - hat * row_mean(up * hat))).astype(BF16)
            sec_scr[k] = grad_b
            total_b = total_b + grad_b.astype(F32)
            grad_a = dot_back(grad_b, w_second_ref[...]) * slope_scr[now, k].astype(F32)
            grad_a = grad_a.astype(BF16)
            grad_a_ref[k] = grad_a
            total_a = total_a + grad_a.astype(F32)
        flat = degree * block
        all_a = grad_a_ref[...].reshape(flat, width)
        acc_scr[at_second : at_second + width, :] += dot_rows(
            act_scr[now].reshape(flat, width), sec_scr[...].reshape(flat, width)
        )
        acc_scr[at_first + width : at_first + 2 * width, :] += dot_rows(
            snd_scr[now].reshape(flat, width), all_a
        )
        acc_scr[at_first + 2 * width : at_first + 3 * width, :] += dot_rows(
            edges_ref[...].reshape(flat, width), all_a
        )
        received = total_a.astype(BF16)
        acc_scr[at_first : at_first + width, :] += dot_rows(nodes_ref[here, :], received)
        grad_nodes_ref[here, :] += dot_back(received, w_first_ref[:width, :])
        acc_scr[at_vec : at_vec + 1, :] += col_sum(total_a)
        acc_scr[at_vec + 1 : at_vec + 2, :] += col_sum(total_b)

    @pl.when(step == 2 * blocks - 1)
    def hand_over():
        place = place_ref[0]
        half = keep_ref.shape[0] // part_rows
        for p in range(2 * half):
            start = pl.multiple_of((place ^ p) * part_rows, 16)
            piece = acc_scr[pl.ds(start, part_rows), :]
            if p < half:
                keep_ref[p * part_rows : (p + 1) * part_rows, :] = piece
            else:
                out = (p - half) * part_rows
                away_ref[out : out + part_rows, :] = piece.astype(BF16)


def main(place, index, valid, edges, own, nodes, halo, cot, vec, w1, w2, n1, n2, parts):
    degree, rows, width = edges.shape
    blocks = rows // BLOCK
    grad_rows = w1.shape[0] + w2.shape[0] + n1.shape[0] + n2.shape[0] + 8
    part_rows = -(-grad_rows // (16 * parts)) * 16
    total = part_rows * parts

    def blocked(first):
        return lambda i, *_: first(jnp.where(i < blocks, i, i - blocks))

    def whole(array):
        zeros = (0,) * array.ndim
        return pl.BlockSpec(array.shape, lambda i, *_: zeros, pipeline_mode=pl.Buffered(1))

    edge_spec = pl.BlockSpec((degree, BLOCK, width), blocked(lambda i: (0, i, 0)))
    flag_spec = pl.BlockSpec((degree, BLOCK), blocked(lambda i: (0, i)))
    own_spec = pl.BlockSpec(
        (degree, BLOCK, width), lambda i, *_: (0, jnp.minimum(i, blocks - 1), 0)
    )
    out_spec = pl.BlockSpec(
        (degree, BLOCK, width), lambda i, *_: (0, jnp.maximum(i - blocks, 0), 0)
    )
    half = jax.ShapeDtypeStruct((total // 2, width), BF16)
    keep = jax.ShapeDtypeStruct((total // 2, width), F32)
    grid_spec = pltpu.PrefetchScalarGridSpec(
        num_scalar_prefetch=1,
        grid=(2 * blocks,),
        in_specs=[flag_spec, flag_spec, edge_spec, own_spec]
        + [whole(a) for a in (nodes, halo, cot, vec, w1, w2, n1, n2)],
        out_specs=(whole(nodes), whole(nodes), out_spec, whole(half), whole(keep)),
        scratch_shapes=[
            pltpu.VMEM((blocks, degree, BLOCK, width), BF16),
            pltpu.VMEM((blocks, degree, BLOCK, width), BF16),
            pltpu.VMEM((blocks, degree, BLOCK, width), BF16),
            pltpu.VMEM((blocks, degree, BLOCK, width), BF16),
            pltpu.VMEM((blocks, degree, BLOCK, LANES), F32),
            pltpu.VMEM((rows, width), F32),
            pltpu.VMEM((rows, LANES), F32),
            pltpu.VMEM((rows, width), F32),
            pltpu.VMEM((degree, BLOCK, width), BF16),
            pltpu.VMEM((total, width), F32),
        ],
    )
    return pl.pallas_call(
        functools.partial(main_kernel, blocks, part_rows),
        grid_spec=grid_spec,
        out_shape=(
            jax.ShapeDtypeStruct((rows, width), BF16),
            jax.ShapeDtypeStruct((rows, width), F32),
            jax.ShapeDtypeStruct((degree, rows, width), BF16),
            half,
            keep,
        ),
        compiler_params=params(),
        cost_estimate=cost(18 * degree * rows * width * width, 8 * edges.size),
        name="edges_and_nodes",
    )(place, index, valid, edges, own, nodes, halo, cot, vec, w1, w2, n1, n2)


def split_back(total, weight):
    high = total.astype(BF16)
    low = (total - high.astype(F32)).astype(BF16)
    return dot_back(high, weight) + dot_back(low, weight)


def spread_kernel(first, index_ref, grad_ref, weight_ref, *rest):
    *extra, out_ref, total = rest
    step = pl.program_id(0)
    degree, block, width = grad_ref.shape
    rows = total.shape[0]
    index = index_ref[...]
    hot = jnp.concatenate(
        [hot_rows(index[k : k + 1, :], first, rows) for k in range(degree)], axis=1
    )
    part = dot(hot, grad_ref[...].reshape(degree * block, width))

    @pl.when(step == 0)
    def start():
        total[...] = part

    @pl.when(step > 0)
    def go_on():
        total[...] += part

    @pl.when(step == pl.num_programs(0) - 1)
    def finish():
        result = split_back(total[...], weight_ref[...])
        if extra:
            result = result + extra[0][...]
        out_ref[...] = result.astype(out_ref.dtype)


def spread(index, grad, weight, first, rows, dtype, extra=None):
    degree, count, width = grad.shape
    base = []
    if extra is not None:
        base = [pl.BlockSpec((rows, width), lambda i: (first // rows, 0))]
    return pl.pallas_call(
        functools.partial(spread_kernel, first),
        grid=(count // BLOCK,),
        in_specs=[
            pl.BlockSpec((degree, BLOCK), lambda i: (0, i)),
            pl.BlockSpec((degree, BLOCK, width), lambda i: (0, i, 0)),
            pl.BlockSpec(weight.shape, lambda i: (0, 0)),
        ]
        + base,
        out_specs=pl.BlockSpec((rows, width), lambda i: (0, 0)),
        out_shape=jax.ShapeDtypeStruct((rows, width), dtype),
        scratch_shapes=[pltpu.VMEM((rows, width), F32)],
        compiler_params=params(),
        cost_estimate=cost(2 * rows * grad.size, 2 * grad.size),
        name="spread_rows",
    )(index, grad, weight, *([] if extra is None else [extra]))


def edge_kernel(grad_ref, weight_ref, out_ref):
    degree, block, width = grad_ref.shape
    grad = grad_ref[...].reshape(degree * block, width)
    out_ref[...] = dot_back(grad, weight_ref[...]).astype(BF16).reshape(degree, block, width)


def edge_grads(grad, weight):
    degree, count, width = grad.shape
    spec = pl.BlockSpec((degree, BLOCK, width), lambda i: (0, i, 0))
    return pl.pallas_call(
        edge_kernel,
        grid=(count // BLOCK,),
        in_specs=[spec, pl.BlockSpec(weight.shape, lambda i: (0, 0))],
        out_specs=spec,
        out_shape=jax.ShapeDtypeStruct(grad.shape, BF16),
        compiler_params=params(),
        cost_estimate=cost(2 * grad.size * width, 4 * grad.size),
        name="edge_grads",
    )(grad, weight)


def final_kernel(lists_ref, low_ref, high_ref, next_ref, prev_ref, out_ref):
    rows = out_ref.shape[0]
    low = low_ref.shape[0]
    for first, part_ref in ((0, low_ref), (low, high_ref)):
        count = part_ref.shape[0]
        out_ref[first : first + count, :] = (
            part_ref[...]
            + dot(hot_rows(lists_ref[0:1, :], first, count), next_ref[...])
            + dot(hot_rows(lists_ref[1:2, :], first, count), prev_ref[...])
        )


def final(lists, low, high, ret_next, ret_prev):
    rows = low.shape[0] + high.shape[0]
    width = low.shape[1]
    return pl.pallas_call(
        final_kernel,
        out_shape=jax.ShapeDtypeStruct((rows, width), F32),
        compiler_params=params(),
        cost_estimate=cost(4 * rows * ret_next.size, 8 * rows * width),
        name="returned_rows",
    )(lists, low, high, ret_next, ret_prev)


def add_kernel(keep_ref, came_ref, away_ref, out_ref):
    half = out_ref.shape[0]
    out_ref[...] = keep_ref[:half, :] + came_ref[:half, :].astype(F32)
    away_ref[...] = (keep_ref[half:, :] + came_ref[half:, :].astype(F32)).astype(BF16)


def add_and_split(keep, came):
    half, width = keep.shape[0] // 2, keep.shape[1]
    return pl.pallas_call(
        add_kernel,
        out_shape=(
            jax.ShapeDtypeStruct((half, width), BF16),
            jax.ShapeDtypeStruct((half, width), F32),
        ),
        compiler_params=params(),
        cost_estimate=cost(keep.size, 8 * keep.size),
        name="add_and_split",
    )(keep, came)


def unpack_kernel(part_rows, place_ref, *refs):
    pieces, outs, full = refs[:4], refs[4:-1], refs[-1]
    place = place_ref[0]
    p = 0
    for piece in pieces:
        for at in range(0, piece.shape[0], part_rows):
            start = pl.multiple_of((place ^ p) * part_rows, 16)
            full[pl.ds(start, part_rows), :] = piece[at : at + part_rows, :].astype(F32)
            p += 1
    at = 0
    for out_ref in outs:
        count = out_ref.shape[0]
        out_ref[...] = full[at : at + count, :]
        at += count


def unpack(place, pieces, row_counts):
    part_rows, width = pieces[0].shape
    total = 8 * part_rows
    return pl.pallas_call(
        functools.partial(unpack_kernel, part_rows),
        in_specs=[pl.BlockSpec(memory_space=pltpu.SMEM)]
        + [pl.BlockSpec(memory_space=pltpu.VMEM)] * 4,
        out_shape=tuple(jax.ShapeDtypeStruct((n, width), F32) for n in row_counts),
        scratch_shapes=[pltpu.VMEM((total, width), F32)],
        compiler_params=params(),
        name="unpack_sums",
    )(place, *pieces)


def traded(value, mask):
    count = lax.axis_size("face") * lax.axis_size("sub")
    return lax.ppermute(value, BOTH, [(i, i ^ mask) for i in range(count)])


def passed_along(value, steps):
    count = lax.axis_size("face")
    pairs = [(source, (source + steps) % count) for source in range(count)]
    return lax.ppermute(value, "face", pairs)


def body(
    nodes,
    edges,
    neighbours,
    valid,
    send_lists,
    edge_first,
    edge_first_bias,
    edge_second,
    edge_second_bias,
    edge_gain,
    edge_shift,
    node_first,
    node_first_bias,
    node_second,
    node_second_bias,
    node_gain,
    node_shift,
    cotangent,
):
    rows, width = nodes.shape
    lists = send_lists[0]
    halo_rows = lists.shape[1]
    index = neighbours.T
    flags = valid.T
    edge_rows = jnp.transpose(edges, (1, 0, 2))
    vec = jnp.stack(
        [
            edge_first_bias,
            edge_second_bias,
            edge_gain,
            edge_shift,
            node_first_bias,
            node_second_bias,
            node_gain,
            node_shift,
        ]
    ).astype(F32)
    subs = lax.axis_size("sub")
    me = lax.axis_index("face") * subs + lax.axis_index("sub")
    devices = lax.axis_size("face") * subs
    masks = [1 << b for b in range(devices.bit_length() - 1)]
    masks = [subs] + [m for m in masks if m != subs]
    halving, doubling = masks[:3], masks[3:]
    place = jnp.int32(0)
    for mask in halving:
        place = place * 2 + jnp.where((me & mask) != 0, 1, 0)
    place = place.astype(jnp.int32).reshape(1)

    to_next, to_prev = pick(lists, nodes)
    from_prev = passed_along(to_next, 1)
    from_next = passed_along(to_prev, -1)
    own = own_senders(index, nodes)
    halo = jnp.concatenate([from_prev, from_next], axis=0)
    mixed, grad_nodes, grad_a, away, keep = main(
        place,
        index,
        flags,
        edge_rows,
        own,
        nodes,
        halo,
        cotangent,
        vec,
        edge_first,
        edge_second,
        node_first,
        node_second,
        1 << len(halving),
    )
    send_weight = edge_first[width : 2 * width]
    edge_weight = edge_first[2 * width :]

    came = traded(away, halving[0])
    for mask in halving[1:]:
        away, keep = add_and_split(keep, came)
        came = traded(away, mask)
    part = (keep + came.astype(F32)).astype(BF16)
    for mask in doubling:
        part = (part.astype(F32) + traded(part, mask).astype(F32)).astype(BF16)

    back = spread(index, grad_a, send_weight, rows, 2 * halo_rows, BF16)
    ret_next = passed_along(back[:halo_rows], -1)
    ret_prev = passed_along(back[halo_rows:], 1)
    half = rows // 2
    low = spread(index, grad_a, send_weight, 0, half, F32, grad_nodes)
    high = spread(index, grad_a, send_weight, half, half, F32, grad_nodes)
    grad_edges = edge_grads(grad_a, edge_weight)
    grad_nodes = final(lists, low, high, ret_next, ret_prev)

    pieces = [part]
    held = part
    for mask in halving[::-1]:
        came = traded(held, mask)
        pieces.append(came)
        held = jnp.concatenate([held, came], axis=0)
    counts = (edge_first.shape[0], width, node_first.shape[0], width) + (1,) * 8
    sums = unpack(place, pieces, counts)
    vectors = [v.reshape(width) for v in sums[4:]]
    return (
        mixed,
        grad_nodes,
        jnp.transpose(grad_edges, (1, 0, 2)),
        sums[0],
        vectors[0],
        sums[1],
        vectors[1],
        vectors[2],
        vectors[3],
        sums[2],
        vectors[4],
        sums[3],
        vectors[5],
        vectors[6],
        vectors[7],
    )


def solution(mesh):
    shared = P(("face", "sub"), None)
    split3 = P(("face", "sub"), None, None)
    return jax.shard_map(
        body,
        mesh=mesh,
        in_specs=(shared, split3, shared, shared, split3) + (P(),) * 12 + (shared,),
        out_specs=(shared, shared, split3) + (P(),) * 12,
        check_vma=False,
    )
```

```python
import functools

import jax
import jax.numpy as jnp
from jax import lax
from jax.experimental import pallas as pl
from jax.experimental.pallas import tpu as pltpu
from jax.sharding import PartitionSpec as P

F32 = jnp.float32
BF16 = jnp.bfloat16
LANES = 128
BLOCK = 128
PARTS = 5
PARTS2 = 5
CHUNK = 64
BOTH = ("face", "sub")
MIB = 1024 * 1024
VMEM_LIMIT = 30 * MIB


def params(limit=VMEM_LIMIT):
    return pltpu.CompilerParams(vmem_limit_bytes=limit)


def cost(flops, moved):
    return pl.CostEstimate(flops=int(flops), bytes_accessed=int(moved), transcendentals=0)


def dot(left, right):
    return jnp.dot(left, right, preferred_element_type=F32)


def dot_rows(left, right):
    return lax.dot_general(left, right, (((0,), (0,)), ((), ())), preferred_element_type=F32)


def dot_back(left, right):
    return lax.dot_general(left, right, (((1,), (1,)), ((), ())), preferred_element_type=F32)


def down(row):
    return jnp.broadcast_to(row, (LANES, LANES)).T


def hot_lanes(index, first, count):
    lane = lax.broadcasted_iota(jnp.int32, (1, LANES), 1)
    index = index.astype(jnp.int16)
    one, zero = BF16(1.0), BF16(0.0)
    tiles = [
        jnp.where(index == (lane + (first + t * LANES)).astype(jnp.int16), one, zero)
        for t in range(count // LANES)
    ]
    return jnp.concatenate(tiles, axis=1)


def hot_rows(index, first, count):
    row = lax.broadcasted_iota(jnp.int32, (count, 1), 0) + first
    return jnp.where(row == index, 1.0, 0.0).astype(BF16)


def row_mean(values):
    return jnp.mean(values, axis=-1, keepdims=True)


def col_sum(values):
    return jnp.sum(values, axis=0, keepdims=True)


def gate(halves):
    twice = 1.0 + jnp.tanh(halves)
    act = halves * twice
    return act, twice + act * (2.0 - twice)


def norm(values):
    centre = values - row_mean(values)
    scale = lax.rsqrt(row_mean(centre * centre) + 1e-05)
    return centre * scale, scale


def pick_kernel(lists_ref, nodes_ref, next_ref, prev_ref):
    rows = nodes_ref.shape[0]
    halo = lists_ref.shape[1]
    for side, out_ref in ((0, next_ref), (1, prev_ref)):
        for at in range(0, halo, LANES):
            index = down(lists_ref[side : side + 1, at : at + LANES])
            out_ref[at : at + LANES, :] = dot(
                hot_lanes(index, 0, rows), nodes_ref[...]
            ).astype(BF16)


def pick(lists, nodes):
    halo, width = lists.shape[1], nodes.shape[1]
    out = jax.ShapeDtypeStruct((halo, width), BF16)
    return pl.pallas_call(
        pick_kernel,
        out_shape=(out, out),
        compiler_params=params(),
        cost_estimate=cost(4 * halo * nodes.size, 2 * nodes.size),
        name="pick_rows",
    )(lists, nodes)


def in_vmem(array):
    return pltpu.with_memory_space_constraint(array, pltpu.VMEM)


def own_kernel(index_ref, nodes_ref, out_ref):
    rows = nodes_ref.shape[0]
    k = pl.program_id(0)
    row = index_ref[pl.ds(k, 1), :]
    column = jnp.concatenate(
        [down(row[:, at : at + LANES]) for at in range(0, rows, LANES)], axis=0
    )
    out_ref[0] = dot(hot_lanes(column, 0, rows), nodes_ref[...]).astype(BF16)


def own_senders(index, nodes):
    degree, rows = index.shape
    width = nodes.shape[1]
    return pl.pallas_call(
        own_kernel,
        grid=(degree,),
        in_specs=[pl.BlockSpec(memory_space=pltpu.VMEM)] * 2,
        out_specs=pl.BlockSpec((1, rows, width), lambda i: (i, 0, 0)),
        out_shape=pltpu.HBM((degree, rows, width), BF16),
        compiler_params=params(30 * MIB),
        cost_estimate=cost(2 * degree * rows * rows * width, 2 * degree * rows * width),
        name="own_senders",
    )(index, nodes)


def main_kernel(
    degree,
    part_rows,
    place_ref,
    edges_ref,
    own_ref,
    index_ref,
    valid_ref,
    nodes_ref,
    halo_ref,
    cot_ref,
    vec_ref,
    w_first_ref,
    w_second_ref,
    n_first_ref,
    n_second_ref,
    mixed_ref,
    grad_nodes_ref,
    hat_ref,
    away_ref,
    keep_ref,
    snd_ref,
    act_scr,
    slope_scr,
    scale_scr,
    sum_scr,
    count_scr,
    up_scr,
    acc_scr,
    turned_scr,
    half_first,
    half_second,
    bias_scr,
):
    step = pl.program_id(0)
    rows, width = nodes_ref.shape
    e_b1, e_b2, e_gain, e_shift, n_b1, n_b2, n_gain, n_shift = (
        vec_ref[i : i + 1, :] for i in range(8)
    )
    at_first, at_second = 0, 3 * width
    at_nfirst, at_nsecond, at_vec = 4 * width, 6 * width, 7 * width

    def wide(lanes):
        return jnp.concatenate([lanes] * (width // LANES), axis=1)

    @pl.when(step == 0)
    def begin():
        half_first[...] = (w_first_ref[...].astype(F32) * 0.5).astype(BF16)
        half_second[...] = (w_second_ref[...].astype(F32) * 0.5).astype(BF16)
        sum_scr[...] = jnp.zeros(sum_scr.shape, F32)
        count_scr[...] = jnp.zeros(count_scr.shape, F32)
        bias_scr[...] = jnp.zeros(bias_scr.shape, F32)
        acc_scr[...] = jnp.zeros(acc_scr.shape, F32)
        turned_scr[...] = jnp.zeros(turned_scr.shape, F32)
        up_scr[...] = dot(nodes_ref[...], half_first[:width, :]) + 0.5 * e_b1

    @pl.when(step < degree)
    def forward():
        k = step
        joint = index_ref[pl.ds(k, 1), :] * 2 + valid_ref[pl.ds(k, 1), :]
        part = rows // PARTS
        columns, entered = {}, {}

        def choose(p):
            column = jnp.concatenate(
                [down(joint[:, at : at + LANES]) for at in range(p * part, (p + 1) * part, LANES)],
                axis=0,
            )
            columns[p] = column
            return dot(hot_lanes(column >> 1, rows, halo_ref.shape[0]), halo_ref[...])

        def enter(p, picked):
            here = slice(p * part, (p + 1) * part)
            snd = picked.astype(BF16) + own_ref[0, here, :]
            snd_ref[k, here, :] = snd
            joined = jnp.concatenate([snd, edges_ref[0, here, :]], axis=1)
            return dot(joined, half_first[width:, :])

        def middle(p, pre):
            acts = []
            for at in range(0, part, CHUNK):
                here = slice(p * part + at, p * part + at + CHUNK)
                act, slope = gate(pre[at : at + CHUNK] + up_scr[here, :])
                act = act.astype(BF16)
                acts.append(act)
                act_scr[k, here, :] = act
                slope_scr[k, here, :] = slope.astype(BF16)
            return dot(jnp.concatenate(acts, axis=0), w_second_ref[...])

        def leave(p, second):
            for at in range(0, part, CHUNK):
                here = slice(p * part + at, p * part + at + CHUNK)
                live = (columns[p][at : at + CHUNK] & 1).astype(F32)
                value = second[at : at + CHUNK] + e_b2
                centre = value - row_mean(value)
                scale = lax.rsqrt(row_mean(centre * centre) + 1e-05) * live
                hat = centre * wide(scale)
                hat_ref[k, here, :] = hat.astype(BF16)
                scale_scr[k, here, :] = scale.astype(scale_scr.dtype)
                sum_scr[here, :] += hat
                count_scr[here, :] += live

        chosen, seconds = {}, {}
        for i in range(PARTS):
            chosen[i] = choose(i)
        for i in range(PARTS):
            entered[i] = enter(i, chosen.pop(i))
        for i in range(PARTS):
            seconds[i] = middle(i, entered.pop(i))
        for i in range(PARTS):
            leave(i, seconds.pop(i))

    @pl.when(step == degree)
    def node_stage():
        part = rows // PARTS
        parts = [slice(p * part, (p + 1) * part) for p in range(PARTS)]
        gathered, firsts, acts, slopes, seconds = [], [], [], [], []
        hats, grads_d, grads_c, backs = [], [], [], []
        for here in parts:
            counts = wide(count_scr[here, :])
            gathered.append((sum_scr[here, :] * e_gain + counts * e_shift).astype(BF16))
            joined = jnp.concatenate([nodes_ref[here, :], gathered[-1]], axis=1)
            firsts.append(dot(joined, n_first_ref[...]))
        for first in firsts:
            act, slope = gate(0.5 * (first + n_b1))
            acts.append(act.astype(BF16))
            slopes.append(0.5 * slope)
            seconds.append(dot(acts[-1], n_second_ref[...]))
        ups, hat_sums, up_sums, d_sums, c_sums = [], [], [], [], []
        for here, second in zip(parts, seconds):
            hat, scale = norm(second + n_b2)
            out = nodes_ref[here, :].astype(F32) + (hat * n_gain + n_shift)
            mixed_ref[here, :] = out.astype(BF16)
            up = cot_ref[here, :].astype(F32)
            hat_sums.append(col_sum(up * hat))
            up_sums.append(col_sum(up))
            scaled = up * n_gain
            grad = scale * (scaled - row_mean(scaled) - hat * row_mean(scaled * hat))
            d_sums.append(col_sum(grad))
            grads_d.append(grad.astype(BF16))
            backs.append(dot_back(grads_d[-1], n_second_ref[...]))
        for p in range(PARTS):
            grad = backs[p] * slopes[p]
            c_sums.append(col_sum(grad))
            grads_c.append(grad.astype(BF16))
        all_d, all_c = jnp.concatenate(grads_d, axis=0), jnp.concatenate(grads_c, axis=0)
        acc_scr[at_nsecond : at_nsecond + width, :] = dot_rows(
            jnp.concatenate(acts, axis=0), all_d
        )
        for p, here in enumerate(parts):
            gain_part = dot_back(grads_c[p], n_first_ref[width:, :])
            own_part = dot_back(grads_c[p], n_first_ref[:width, :])
            grad_nodes_ref[here, :] = cot_ref[here, :].astype(F32) + own_part
            sums, counts = sum_scr[here, :], wide(count_scr[here, :])
            acc_scr[at_vec + 2 : at_vec + 3, :] += col_sum(gain_part * sums)
            acc_scr[at_vec + 3 : at_vec + 4, :] += col_sum(gain_part * counts)
            scaled = gain_part * e_gain
            up_scr[here, :] = scaled - row_mean(scaled)
            sum_scr[here, :] = jnp.zeros((part, width), F32)
        acc_scr[at_nfirst : at_nfirst + width, :] = dot_rows(nodes_ref[...], all_c)
        acc_scr[at_nfirst + width : at_nfirst + 2 * width, :] = dot_rows(
            jnp.concatenate(gathered, axis=0), all_c
        )
        for row, values in ((4, c_sums), (5, d_sums), (6, hat_sums), (7, up_sums)):
            acc_scr[at_vec + row : at_vec + row + 1, :] = sum(values)

    def outer(k):
        all_a = hat_ref[k]
        turned_scr[:, :width] += dot_rows(all_a, snd_ref[k])
        turned_scr[:, width:] += dot_rows(all_a, edges_ref[0])

    def backward(k):
        part = rows // PARTS2
        grads, backs = [], []
        for p in range(PARTS2):
            out = []
            for at in range(p * part, (p + 1) * part, CHUNK):
                here = slice(at, at + CHUNK)
                hat = hat_ref[k, here, :].astype(F32)
                scale = wide(scale_scr[k, here, :].astype(F32))
                up = up_scr[here, :]
                grad = scale * (up - hat * row_mean(up * hat))
                bias_scr[...] += jnp.sum(grad.reshape(CHUNK // 8, 8, width), axis=0)
                out.append(grad.astype(BF16))
            grads.append(jnp.concatenate(out, axis=0))
            backs.append(dot_back(grads[-1], half_second[...]))
        acc_scr[at_second : at_second + width, :] += dot_rows(
            act_scr[k], jnp.concatenate(grads, axis=0)
        )
        for p in range(PARTS2):
            for at in range(0, part, CHUNK):
                here = slice(p * part + at, p * part + at + CHUNK)
                grad = backs[p][at : at + CHUNK] * slope_scr[k, here, :].astype(F32)
                sum_scr[here, :] += grad
                hat_ref[k, here, :] = grad.astype(BF16)

    @pl.when(step == degree)
    def first_back():
        backward(0)

    @pl.when((step > degree) & (step < 2 * degree))
    def go_back():
        outer(step - degree - 1)
        backward(step - degree)

    @pl.when(step == 2 * degree)
    def hand_over():
        outer(degree - 1)
        acc_scr[at_vec + 1 : at_vec + 2, :] = col_sum(bias_scr[...])
        acc_scr[at_vec : at_vec + 1, :] = col_sum(sum_scr[...])
        received = sum_scr[...].astype(BF16)
        acc_scr[at_first : at_first + width, :] = dot_rows(nodes_ref[...], received)
        grad_nodes_ref[...] += dot_back(received, w_first_ref[:width, :])
        acc_scr[at_first + width : at_first + 3 * width, :] = turned_scr[...].T
        place = place_ref[0]
        half = keep_ref.shape[0] // part_rows
        for p in range(2 * half):
            start = pl.multiple_of((place ^ p) * part_rows, 16)
            piece = acc_scr[pl.ds(start, part_rows), :]
            if p < half:
                keep_ref[p * part_rows : (p + 1) * part_rows, :] = piece
            else:
                out = (p - half) * part_rows
                away_ref[out : out + part_rows, :] = piece.astype(BF16)


def main(place, index, valid, edges, own, nodes, halo, cot, vec, w1, w2, n1, n2, parts):
    degree, rows, width = edges.shape
    grad_rows = w1.shape[0] + w2.shape[0] + n1.shape[0] + n2.shape[0] + 8
    part_rows = -(-grad_rows // (16 * parts)) * 16
    total = part_rows * parts
    resident = pl.BlockSpec(memory_space=pltpu.VMEM)
    edge_spec = pl.BlockSpec((1, rows, width), lambda i, *_: (jnp.where(i > degree, i - degree - 1, jnp.minimum(i, degree - 1)), 0, 0))
    held = (index, valid, nodes, halo, cot, vec, w1, w2, n1, n2)
    own_spec = pl.BlockSpec(
        (1, rows, width), lambda i, *_: (jnp.minimum(i, degree - 1), 0, 0)
    )
    grid_spec = pltpu.PrefetchScalarGridSpec(
        num_scalar_prefetch=1,
        grid=(2 * degree + 1,),
        in_specs=[edge_spec, own_spec] + [resident] * len(held),
        out_specs=[resident] * 5,
        scratch_shapes=[
            pltpu.VMEM((degree, rows, width), BF16),
            pltpu.VMEM((degree, rows, width), BF16),
            pltpu.VMEM((degree, rows, width), BF16),
            pltpu.VMEM((degree, rows, LANES), BF16),
            pltpu.VMEM((rows, width), F32),
            pltpu.VMEM((rows, LANES), F32),
            pltpu.VMEM((rows, width), F32),
            pltpu.VMEM((total, width), F32),
            pltpu.VMEM((width, 2 * width), F32),
            pltpu.VMEM(w1.shape, BF16),
            pltpu.VMEM(w2.shape, BF16),
            pltpu.VMEM((8, width), F32),
        ],
    )
    return pl.pallas_call(
        functools.partial(main_kernel, degree, part_rows),
        grid_spec=grid_spec,
        out_shape=(
            pltpu.VMEM((rows, width), BF16),
            pltpu.VMEM((rows, width), F32),
            pltpu.VMEM((degree, rows, width), BF16),
            pltpu.VMEM((total // 2, width), BF16),
            pltpu.VMEM((total // 2, width), F32),
        ),
        compiler_params=params(46 * MIB),
        cost_estimate=cost(18 * degree * rows * width * width, 8 * edges.size),
        name="edges_and_nodes",
    )(place, edges, pltpu.with_memory_space_constraint(own, pltpu.HBM), *held)


def split_back(total, weight):
    high = total.astype(BF16)
    low = (total - high.astype(F32)).astype(BF16)
    return dot_back(high, weight) + dot_back(low, weight)


def spread_kernel(first, index_ref, grad_ref, weight_ref, *rest):
    *extra, out_ref, total = rest
    degree = grad_ref.shape[0]
    rows = total.shape[0]
    k = pl.program_id(0) * 2
    hots = [hot_rows(index_ref[pl.ds(k + j, 1), :], first, rows) for j in range(2)]
    count, width = grad_ref.shape[1:]
    part = dot(
        jnp.concatenate(hots, axis=1),
        grad_ref[pl.ds(k, 2)].reshape(2 * count, width),
    )

    @pl.when(k == 0)
    def start():
        total[...] = part

    @pl.when(k > 0)
    def go_on():
        total[...] += part

    @pl.when(k == degree - 2)
    def finish():
        result = split_back(total[...], weight_ref[...])
        if extra:
            result = result + extra[0][first : first + rows, :]
        out_ref[...] = result.astype(out_ref.dtype)


def spread(index, grad, weight, first, rows, dtype, extra=None):
    degree, count, width = grad.shape
    resident = pl.BlockSpec(memory_space=pltpu.VMEM)
    held = [index, grad, weight] + ([] if extra is None else [extra])
    return pl.pallas_call(
        functools.partial(spread_kernel, first),
        grid=(degree // 2,),
        in_specs=[resident] * len(held),
        out_specs=resident,
        out_shape=pltpu.VMEM((rows, width), dtype),
        scratch_shapes=[pltpu.VMEM((rows, width), F32)],
        compiler_params=params(),
        cost_estimate=cost(2 * rows * grad.size, 2 * grad.size),
        name="spread_rows",
    )(*held)


def edge_kernel(grad_ref, weight_ref, out_ref):
    slots, rows, width = out_ref.shape
    k = pl.program_id(0) * slots
    grad = grad_ref[pl.ds(k, slots)].reshape(slots * rows, width)
    out_ref[...] = dot_back(grad, weight_ref[...]).astype(BF16).reshape(slots, rows, width)


def edge_grads(grad, weight):
    degree, count, width = grad.shape
    resident = pl.BlockSpec(memory_space=pltpu.VMEM)
    return pl.pallas_call(
        edge_kernel,
        grid=(degree // 2,),
        in_specs=[resident, resident],
        out_specs=pl.BlockSpec((2, count, width), lambda i: (i, 0, 0)),
        out_shape=jax.ShapeDtypeStruct(grad.shape, BF16),
        compiler_params=params(),
        cost_estimate=cost(2 * grad.size * width, 4 * grad.size),
        name="edge_grads",
    )(grad, weight)


def final_kernel(lists_ref, low_ref, high_ref, next_ref, prev_ref, out_ref):
    rows = out_ref.shape[0]
    low = low_ref.shape[0]
    for first, part_ref in ((0, low_ref), (low, high_ref)):
        count = part_ref.shape[0]
        out_ref[first : first + count, :] = (
            part_ref[...]
            + dot(hot_rows(lists_ref[0:1, :], first, count), next_ref[...])
            + dot(hot_rows(lists_ref[1:2, :], first, count), prev_ref[...])
        )


def final(lists, low, high, ret_next, ret_prev):
    rows = low.shape[0] + high.shape[0]
    width = low.shape[1]
    return pl.pallas_call(
        final_kernel,
        out_shape=jax.ShapeDtypeStruct((rows, width), F32),
        compiler_params=params(),
        cost_estimate=cost(4 * rows * ret_next.size, 8 * rows * width),
        name="returned_rows",
    )(lists, low, high, ret_next, ret_prev)


def split_kernel(keep_ref, came_ref, own_ref, *away_refs):
    part = own_ref.shape[0]
    for p, out_ref in enumerate((own_ref,) + away_refs):
        here = slice(p * part, (p + 1) * part)
        total = keep_ref[here, :] + came_ref[here, :].astype(F32)
        out_ref[...] = total.astype(out_ref.dtype)


def add_and_split(keep, came):
    part, width = keep.shape[0] // 4, keep.shape[1]
    return pl.pallas_call(
        split_kernel,
        out_shape=(pltpu.VMEM((part, width), F32),) + (pltpu.VMEM((part, width), BF16),) * 3,
        compiler_params=params(),
        cost_estimate=cost(keep.size, 8 * keep.size),
        name="add_and_split",
    )(keep, came)


def sum_kernel(own_ref, *refs):
    *came, out_ref = refs
    values = [own_ref[...].astype(F32)] + [r[...].astype(F32) for r in came]
    while len(values) > 1:
        values = [a + b for a, b in zip(values[::2], values[1::2])]
    out_ref[...] = values[0].astype(BF16)


def sum_parts(own, came):
    return pl.pallas_call(
        sum_kernel,
        out_shape=pltpu.VMEM(own.shape, BF16),
        compiler_params=params(),
        cost_estimate=cost(own.size * len(came), 8 * own.size),
        name="sum_parts",
    )(own, *came)


def unpack_kernel(part_rows, place_ref, *refs):
    pieces, outs, full = refs[:5], refs[5:-1], refs[-1]
    place = place_ref[0]
    p = 0
    for piece in pieces:
        for at in range(0, piece.shape[0], part_rows):
            start = pl.multiple_of((place ^ p) * part_rows, 16)
            full[pl.ds(start, part_rows), :] = piece[at : at + part_rows, :].astype(F32)
            p += 1
    at = 0
    for out_ref in outs:
        count = out_ref.shape[0]
        out_ref[...] = full[at : at + count, :]
        at += count


def unpack(place, pieces, row_counts):
    part_rows, width = pieces[0].shape
    total = 8 * part_rows
    return pl.pallas_call(
        functools.partial(unpack_kernel, part_rows),
        in_specs=[pl.BlockSpec(memory_space=pltpu.SMEM)]
        + [pl.BlockSpec(memory_space=pltpu.VMEM)] * 5,
        out_shape=tuple(jax.ShapeDtypeStruct((n, width), F32) for n in row_counts),
        scratch_shapes=[pltpu.VMEM((total, width), F32)],
        compiler_params=params(),
        name="unpack_sums",
    )(place, *pieces)


def traded(value, mask):
    count = lax.axis_size("face") * lax.axis_size("sub")
    return lax.ppermute(value, BOTH, [(i, i ^ mask) for i in range(count)])


def tied(*values):
    return lax.optimization_barrier(values)


def passed_along(value, steps):
    count = lax.axis_size("face")
    pairs = [(source, (source + steps) % count) for source in range(count)]
    return lax.ppermute(value, "face", pairs)


def body(
    nodes,
    edges,
    neighbours,
    valid,
    send_lists,
    edge_first,
    edge_first_bias,
    edge_second,
    edge_second_bias,
    edge_gain,
    edge_shift,
    node_first,
    node_first_bias,
    node_second,
    node_second_bias,
    node_gain,
    node_shift,
    cotangent,
):
    rows, width = nodes.shape
    lists = send_lists[0]
    halo_rows = lists.shape[1]
    index = neighbours.T
    flags = valid.T
    edge_rows = jnp.transpose(edges, (1, 0, 2))
    vec = jnp.stack(
        [
            edge_first_bias,
            edge_second_bias,
            edge_gain,
            edge_shift,
            node_first_bias,
            node_second_bias,
            node_gain,
            node_shift,
        ]
    ).astype(F32)
    subs = lax.axis_size("sub")
    me = lax.axis_index("face") * subs + lax.axis_index("sub")
    devices = lax.axis_size("face") * subs
    masks = [1 << b for b in range(devices.bit_length() - 1)]
    masks = [subs] + [m for m in masks if m != subs]
    halving, doubling = masks[:3], masks[3:]
    place = jnp.int32(0)
    for mask in halving:
        place = place * 2 + jnp.where((me & mask) != 0, 1, 0)
    place = place.astype(jnp.int32).reshape(1)

    nodes_held, index_held = in_vmem(nodes), in_vmem(index)
    to_next, to_prev = pick(in_vmem(lists), nodes_held)
    from_prev = passed_along(to_next, 1)
    from_next = passed_along(to_prev, -1)
    own = own_senders(index_held, nodes_held)
    halo = jnp.concatenate([from_prev, from_next], axis=0)
    weights = [in_vmem(a) for a in (edge_first, edge_second, node_first, node_second)]
    mixed, grad_nodes, grad_a, away, keep = main(
        place,
        index_held,
        in_vmem(flags),
        edge_rows,
        own,
        nodes_held,
        in_vmem(halo),
        in_vmem(cotangent),
        in_vmem(vec),
        *weights,
        1 << len(halving),
    )
    send_weight = edge_first[width : 2 * width]
    edge_weight = edge_first[2 * width :]
    half = rows // 2
    core, outer, inner = halving
    plane = (inner, outer, inner ^ outer)

    came = traded(away, core)
    part, *away = add_and_split(keep, came)
    came = [traded(a, mask) for a, mask in zip(away, plane)]
    grad_a, part = tied(grad_a, part)
    back = spread(index_held, grad_a, send_weight, rows, 2 * halo_rows, BF16)
    came, back = tied(came, back)
    part = sum_parts(part, came)
    ret_next = passed_along(back[:halo_rows], -1)
    ret_prev = passed_along(back[halo_rows:], 1)
    while doubling:
        first, *doubling = doubling
        group = [first]
        if doubling:
            second, *doubling = doubling
            group = [first, second, first ^ second]
        came = [traded(part, mask) for mask in group]
        if not doubling:
            grad_a, part = tied(grad_a, part)
            low = spread(index_held, grad_a, send_weight, 0, half, F32, grad_nodes)
            came, low = tied(came, low)
        part = sum_parts(part, came)
    came = [traded(part, mask) for mask in plane]
    grad_a, part = tied(grad_a, part)
    high = spread(index_held, grad_a, send_weight, half, half, F32, grad_nodes)
    came, high = tied(came, high)
    pieces = [part] + came
    pieces.append(traded(jnp.concatenate(pieces, axis=0), core))
    grad_edges = edge_grads(grad_a, edge_weight)
    grad_nodes = final(lists, low, high, ret_next, ret_prev)
    counts = (edge_first.shape[0], width, node_first.shape[0], width) + (1,) * 8
    sums = unpack(place, pieces, counts)
    vectors = [v.reshape(width) for v in sums[4:]]
    return (
        mixed,
        grad_nodes,
        jnp.transpose(grad_edges, (1, 0, 2)),
        sums[0],
        vectors[0],
        sums[1],
        vectors[1],
        vectors[2],
        vectors[3],
        sums[2],
        vectors[4],
        sums[3],
        vectors[5],
        vectors[6],
        vectors[7],
    )


def solution(mesh):
    shared = P(("face", "sub"), None)
    split3 = P(("face", "sub"), None, None)
    return jax.shard_map(
        body,
        mesh=mesh,
        in_specs=(shared, split3, shared, shared, split3) + (P(),) * 12 + (shared,),
        out_specs=(shared, shared, split3) + (P(),) * 12,
        check_vma=False,
    )
```

```python
import functools

import jax
import jax.numpy as jnp
from jax import lax
from jax.experimental import pallas as pl
from jax.experimental.pallas import tpu as pltpu
from jax.sharding import PartitionSpec as P

F32 = jnp.float32
BF16 = jnp.bfloat16
LANES = 128
BLOCK = 128
PARTS = 5
PARTS2 = 5
CHUNK = 64
OWN = 3
SPREAD = 6
EDGE = 3
BOTH = ("face", "sub")
MIB = 1024 * 1024
VMEM_LIMIT = 30 * MIB


def params(limit=VMEM_LIMIT):
    return pltpu.CompilerParams(vmem_limit_bytes=limit)


def cost(flops, moved):
    return pl.CostEstimate(flops=int(flops), bytes_accessed=int(moved), transcendentals=0)


def dot(left, right):
    return jnp.dot(left, right, preferred_element_type=F32)


def dot_rows(left, right):
    return lax.dot_general(left, right, (((0,), (0,)), ((), ())), preferred_element_type=F32)


def dot_back(left, right):
    return lax.dot_general(left, right, (((1,), (1,)), ((), ())), preferred_element_type=F32)


def down(row):
    return jnp.broadcast_to(row, (LANES, LANES)).T


def hot_lanes(index, first, count):
    lane = lax.broadcasted_iota(jnp.int32, (1, LANES), 1)
    index = index.astype(jnp.int16)
    one, zero = BF16(1.0), BF16(0.0)
    tiles = [
        jnp.where(index == (lane + (first + t * LANES)).astype(jnp.int16), one, zero)
        for t in range(count // LANES)
    ]
    return jnp.concatenate(tiles, axis=1)


def hot_rows(index, first, count):
    row = lax.broadcasted_iota(jnp.int32, (count, 1), 0) + first
    return jnp.where(row == index, 1.0, 0.0).astype(BF16)


def row_mean(values):
    return jnp.mean(values, axis=-1, keepdims=True)


def col_sum(values):
    return jnp.sum(values, axis=0, keepdims=True)


def gate(halves):
    twice = 1.0 + jnp.tanh(halves)
    act = halves * twice
    return act, twice + act * (2.0 - twice)


def norm(values):
    centre = values - row_mean(values)
    scale = lax.rsqrt(row_mean(centre * centre) + 1e-05)
    return centre * scale, scale


def pick_kernel(
    lists_hbm, nodes_hbm, index_hbm, next_ref, prev_ref, nodes_ref, index_ref, lists_ref, sems
):
    pairs = ((lists_hbm, lists_ref), (nodes_hbm, nodes_ref), (index_hbm, index_ref))
    copies = [pltpu.make_async_copy(a, b, sems.at[i]) for i, (a, b) in enumerate(pairs)]
    for copy in copies:
        copy.start()
    for copy in copies:
        copy.wait()
    rows = nodes_ref.shape[0]
    halo = lists_ref.shape[1]
    for side, out_ref in ((0, next_ref), (1, prev_ref)):
        for at in range(0, halo, LANES):
            picked = down(lists_ref[side : side + 1, at : at + LANES])
            out_ref[at : at + LANES, :] = dot(
                hot_lanes(picked, 0, rows), nodes_ref[...]
            ).astype(BF16)


def in_hbm(array):
    return pltpu.with_memory_space_constraint(array, pltpu.HBM)


def pick(lists, nodes, index):
    halo, width = lists.shape[1], nodes.shape[1]
    out = pltpu.VMEM((halo, width), BF16)
    return pl.pallas_call(
        pick_kernel,
        in_specs=[pl.BlockSpec(memory_space=pltpu.HBM)] * 3,
        out_specs=[pl.BlockSpec(memory_space=pltpu.VMEM)] * 4,
        out_shape=(out, out, pltpu.VMEM(nodes.shape, BF16), pltpu.VMEM(index.shape, jnp.int32)),
        scratch_shapes=[pltpu.VMEM(lists.shape, jnp.int32), pltpu.SemaphoreType.DMA((3,))],
        compiler_params=params(),
        cost_estimate=cost(4 * halo * nodes.size, 2 * nodes.size),
        name="pick_rows",
    )(in_hbm(lists), in_hbm(nodes), in_hbm(index))


def in_vmem(array):
    return pltpu.with_memory_space_constraint(array, pltpu.VMEM)


def own_kernel(index_ref, nodes_ref, out_ref):
    rows = nodes_ref.shape[0]
    slots = out_ref.shape[0]
    for j in range(slots):
        row = index_ref[pl.ds(pl.program_id(0) * slots + j, 1), :]
        column = jnp.concatenate(
            [down(row[:, at : at + LANES]) for at in range(0, rows, LANES)], axis=0
        )
        out_ref[j] = dot(hot_lanes(column, 0, rows), nodes_ref[...]).astype(BF16)


def own_senders(index, nodes):
    degree, rows = index.shape
    width = nodes.shape[1]
    return pl.pallas_call(
        own_kernel,
        grid=(degree // OWN,),
        in_specs=[pl.BlockSpec(memory_space=pltpu.VMEM)] * 2,
        out_specs=pl.BlockSpec((OWN, rows, width), lambda i: (i, 0, 0)),
        out_shape=pltpu.HBM((degree, rows, width), BF16),
        compiler_params=params(30 * MIB),
        cost_estimate=cost(2 * degree * rows * rows * width, 2 * degree * rows * width),
        name="own_senders",
    )(index, nodes)


def main_kernel(
    degree,
    part_rows,
    place_ref,
    edges_ref,
    own_ref,
    index_ref,
    valid_ref,
    nodes_ref,
    halo_ref,
    cot_ref,
    vec_ref,
    w_first_ref,
    w_second_ref,
    n_first_ref,
    n_second_ref,
    mixed_hbm,
    grad_nodes_ref,
    hat_ref,
    away_ref,
    keep_ref,
    snd_ref,
    act_scr,
    slope_scr,
    scale_scr,
    sum_scr,
    count_scr,
    up_scr,
    acc_scr,
    turned_scr,
    half_first,
    half_second,
    bias_scr,
    mixed_ref,
    mixed_sem,
    centred,
):
    step = pl.program_id(0)
    rows, width = nodes_ref.shape
    e_b1, e_b2, e_gain, e_shift, n_b1, n_b2, n_gain, n_shift = (
        vec_ref[i : i + 1, :] for i in range(8)
    )
    at_first, at_second = 0, 3 * width
    at_nfirst, at_nsecond, at_vec = 4 * width, 6 * width, 7 * width

    def wide(lanes):
        return jnp.concatenate([lanes] * (width // LANES), axis=1)

    @pl.when(step == 0)
    def begin():
        half_first[...] = (w_first_ref[...].astype(F32) * 0.5).astype(BF16)
        second = w_second_ref[...].astype(F32)
        half_second[...] = (second * 0.5).astype(BF16)
        centred[...] = (second - row_mean(second)).astype(BF16)
        sum_scr[...] = jnp.zeros(sum_scr.shape, F32)
        count_scr[...] = jnp.zeros(count_scr.shape, F32)
        bias_scr[...] = jnp.zeros(bias_scr.shape, F32)
        acc_scr[...] = jnp.zeros(acc_scr.shape, F32)
        turned_scr[...] = jnp.zeros(turned_scr.shape, F32)
        up_scr[...] = dot(nodes_ref[...], half_first[:width, :]) + 0.5 * e_b1

    @pl.when(step < degree)
    def forward():
        k = step
        joint = index_ref[pl.ds(k, 1), :] * 2 + valid_ref[pl.ds(k, 1), :]
        part = rows // PARTS
        centred_b2 = e_b2 - row_mean(e_b2)
        columns, entered = {}, {}

        def choose(p):
            column = jnp.concatenate(
                [down(joint[:, at : at + LANES]) for at in range(p * part, (p + 1) * part, LANES)],
                axis=0,
            )
            columns[p] = column
            return dot(hot_lanes(column >> 1, rows, halo_ref.shape[0]), halo_ref[...])

        def enter(p, picked):
            here = slice(p * part, (p + 1) * part)
            snd = picked.astype(BF16) + own_ref[0, here, :]
            snd_ref[k, here, :] = snd
            joined = jnp.concatenate([snd, edges_ref[0, here, :]], axis=1)
            return dot(joined, half_first[width:, :])

        def middle(p, pre):
            acts = []
            for at in range(0, part, CHUNK):
                here = slice(p * part + at, p * part + at + CHUNK)
                act, slope = gate(pre[at : at + CHUNK] + up_scr[here, :])
                act = act.astype(BF16)
                acts.append(act)
                act_scr[k, here, :] = act
                slope_scr[k, here, :] = slope.astype(BF16)
            return dot(jnp.concatenate(acts, axis=0), centred[...])

        def leave(p, second):
            for at in range(0, part, CHUNK):
                here = slice(p * part + at, p * part + at + CHUNK)
                live = (columns[p][at : at + CHUNK] & 1).astype(F32)
                centre = second[at : at + CHUNK] + centred_b2
                scale = lax.rsqrt(row_mean(centre * centre) + 1e-05) * live
                hat = centre * wide(scale)
                hat_ref[k, here, :] = hat.astype(BF16)
                scale_scr[k, here, :] = scale.astype(scale_scr.dtype)
                sum_scr[here, :] += hat
                count_scr[here, :] += live

        chosen, seconds = {}, {}
        for i in range(PARTS):
            chosen[i] = choose(i)
        for i in range(PARTS):
            entered[i] = enter(i, chosen.pop(i))
        for i in range(PARTS):
            seconds[i] = middle(i, entered.pop(i))
        for i in range(PARTS):
            leave(i, seconds.pop(i))

    @pl.when(step == degree)
    def node_stage():
        part = rows // PARTS
        parts = [slice(p * part, (p + 1) * part) for p in range(PARTS)]
        gathered, firsts, acts, slopes, seconds = [], [], [], [], []
        hats, grads_d, grads_c, backs = [], [], [], []
        for here in parts:
            counts = wide(count_scr[here, :])
            gathered.append((sum_scr[here, :] * e_gain + counts * e_shift).astype(BF16))
            joined = jnp.concatenate([nodes_ref[here, :], gathered[-1]], axis=1)
            firsts.append(dot(joined, n_first_ref[...]))
        for first in firsts:
            act, slope = gate(0.5 * (first + n_b1))
            acts.append(act.astype(BF16))
            slopes.append(0.5 * slope)
            seconds.append(dot(acts[-1], n_second_ref[...]))
        ups, hat_sums, up_sums, d_sums, c_sums = [], [], [], [], []
        for here, second in zip(parts, seconds):
            hat, scale = norm(second + n_b2)
            out = nodes_ref[here, :].astype(F32) + (hat * n_gain + n_shift)
            mixed_ref[here, :] = out.astype(BF16)
            up = cot_ref[here, :].astype(F32)
            hat_sums.append(col_sum(up * hat))
            up_sums.append(col_sum(up))
            scaled = up * n_gain
            grad = scale * (scaled - row_mean(scaled) - hat * row_mean(scaled * hat))
            d_sums.append(col_sum(grad))
            grads_d.append(grad.astype(BF16))
            backs.append(dot_back(grads_d[-1], n_second_ref[...]))
        for p in range(PARTS):
            grad = backs[p] * slopes[p]
            c_sums.append(col_sum(grad))
            grads_c.append(grad.astype(BF16))
        all_d, all_c = jnp.concatenate(grads_d, axis=0), jnp.concatenate(grads_c, axis=0)
        acc_scr[at_nsecond : at_nsecond + width, :] = dot_rows(
            jnp.concatenate(acts, axis=0), all_d
        )
        for p, here in enumerate(parts):
            gain_part = dot_back(grads_c[p], n_first_ref[width:, :])
            own_part = dot_back(grads_c[p], n_first_ref[:width, :])
            grad_nodes_ref[here, :] = cot_ref[here, :].astype(F32) + own_part
            sums, counts = sum_scr[here, :], wide(count_scr[here, :])
            acc_scr[at_vec + 2 : at_vec + 3, :] += col_sum(gain_part * sums)
            acc_scr[at_vec + 3 : at_vec + 4, :] += col_sum(gain_part * counts)
            scaled = gain_part * e_gain
            up_scr[here, :] = scaled - row_mean(scaled)
            sum_scr[here, :] = jnp.zeros((part, width), F32)
        acc_scr[at_nfirst : at_nfirst + width, :] = dot_rows(nodes_ref[...], all_c)
        acc_scr[at_nfirst + width : at_nfirst + 2 * width, :] = dot_rows(
            jnp.concatenate(gathered, axis=0), all_c
        )
        pltpu.make_async_copy(mixed_ref, mixed_hbm, mixed_sem).start()
        for row, values in ((4, c_sums), (5, d_sums), (6, hat_sums), (7, up_sums)):
            acc_scr[at_vec + row : at_vec + row + 1, :] = sum(values)

    def outer(k):
        all_a = hat_ref[k]
        turned_scr[:, :width] += dot_rows(all_a, snd_ref[k])
        turned_scr[:, width:] += dot_rows(all_a, edges_ref[0])

    def backward(k):
        part = rows // PARTS2
        grads, backs = [], []
        for p in range(PARTS2):
            out = []
            for at in range(p * part, (p + 1) * part, CHUNK):
                here = slice(at, at + CHUNK)
                hat = hat_ref[k, here, :].astype(F32)
                scale = wide(scale_scr[k, here, :].astype(F32))
                up = up_scr[here, :]
                grad = scale * (up - hat * row_mean(up * hat))
                bias_scr[...] += jnp.sum(grad.reshape(CHUNK // 8, 8, width), axis=0)
                out.append(grad.astype(BF16))
            grads.append(jnp.concatenate(out, axis=0))
            backs.append(dot_back(grads[-1], half_second[...]))
        acc_scr[at_second : at_second + width, :] += dot_rows(
            act_scr[k], jnp.concatenate(grads, axis=0)
        )
        for p in range(PARTS2):
            for at in range(0, part, CHUNK):
                here = slice(p * part + at, p * part + at + CHUNK)
                grad = backs[p][at : at + CHUNK] * slope_scr[k, here, :].astype(F32)
                sum_scr[here, :] += grad
                hat_ref[k, here, :] = grad.astype(BF16)

    @pl.when(step == degree)
    def first_back():
        backward(0)

    @pl.when((step > degree) & (step < 2 * degree))
    def go_back():
        outer(step - degree - 1)
        backward(step - degree)

    @pl.when(step == 2 * degree)
    def hand_over():
        outer(degree - 1)
        pltpu.make_async_copy(mixed_ref, mixed_hbm, mixed_sem).wait()
        acc_scr[at_vec + 1 : at_vec + 2, :] = col_sum(bias_scr[...])
        acc_scr[at_vec : at_vec + 1, :] = col_sum(sum_scr[...])
        received = sum_scr[...].astype(BF16)
        acc_scr[at_first : at_first + width, :] = dot_rows(nodes_ref[...], received)
        grad_nodes_ref[...] += dot_back(received, w_first_ref[:width, :])
        acc_scr[at_first + width : at_first + 3 * width, :] = turned_scr[...].T
        place = place_ref[0]
        half = keep_ref.shape[0] // part_rows
        for p in range(2 * half):
            start = pl.multiple_of((place ^ p) * part_rows, 16)
            piece = acc_scr[pl.ds(start, part_rows), :]
            if p < half:
                keep_ref[p * part_rows : (p + 1) * part_rows, :] = piece
            else:
                out = (p - half) * part_rows
                away_ref[out : out + part_rows, :] = piece.astype(BF16)


def main(place, index, valid, edges, own, nodes, halo, cot, vec, w1, w2, n1, n2, parts):
    degree, rows, width = edges.shape
    grad_rows = w1.shape[0] + w2.shape[0] + n1.shape[0] + n2.shape[0] + 8
    part_rows = -(-grad_rows // (16 * parts)) * 16
    total = part_rows * parts
    resident = pl.BlockSpec(memory_space=pltpu.VMEM)
    edge_spec = pl.BlockSpec((1, rows, width), lambda i, *_: (jnp.where(i > degree, i - degree - 1, jnp.minimum(i, degree - 1)), 0, 0))
    held = (index, valid, nodes, halo, cot, vec, w1, w2, n1, n2)
    own_spec = pl.BlockSpec(
        (1, rows, width), lambda i, *_: (jnp.minimum(i, degree - 1), 0, 0)
    )
    grid_spec = pltpu.PrefetchScalarGridSpec(
        num_scalar_prefetch=1,
        grid=(2 * degree + 1,),
        in_specs=[edge_spec, own_spec] + [resident] * len(held),
        out_specs=[pl.BlockSpec(memory_space=pltpu.HBM)] + [resident] * 4,
        scratch_shapes=[
            pltpu.VMEM((degree, rows, width), BF16),
            pltpu.VMEM((degree, rows, width), BF16),
            pltpu.VMEM((degree, rows, width), BF16),
            pltpu.VMEM((degree, rows, LANES), BF16),
            pltpu.VMEM((rows, width), F32),
            pltpu.VMEM((rows, LANES), F32),
            pltpu.VMEM((rows, width), F32),
            pltpu.VMEM((total, width), F32),
            pltpu.VMEM((width, 2 * width), F32),
            pltpu.VMEM(w1.shape, BF16),
            pltpu.VMEM(w2.shape, BF16),
            pltpu.VMEM((8, width), F32),
            pltpu.VMEM((rows, width), BF16),
            pltpu.SemaphoreType.DMA,
            pltpu.VMEM(w2.shape, BF16),
        ],
    )
    return pl.pallas_call(
        functools.partial(main_kernel, degree, part_rows),
        grid_spec=grid_spec,
        out_shape=(
            pltpu.HBM((rows, width), BF16),
            pltpu.VMEM((rows, width), F32),
            pltpu.VMEM((degree, rows, width), BF16),
            pltpu.VMEM((total // 2, width), BF16),
            pltpu.VMEM((total // 2, width), F32),
        ),
        compiler_params=params(46 * MIB),
        cost_estimate=cost(18 * degree * rows * width * width, 8 * edges.size),
        name="edges_and_nodes",
    )(place, edges, pltpu.with_memory_space_constraint(own, pltpu.HBM), *held)


def split_back(total, weight):
    high = total.astype(BF16)
    low = (total - high.astype(F32)).astype(BF16)
    return dot_back(high, weight) + dot_back(low, weight)


def spread_kernel(first, index_ref, grad_ref, weight_ref, *rest):
    *base, out_ref, total = rest
    degree, count, width = grad_ref.shape
    rows = total.shape[0]
    step = pl.program_id(0)
    k = step * SPREAD
    hots = [hot_rows(index_ref[pl.ds(k + j, 1), :], first, rows) for j in range(SPREAD)]
    part = dot(
        jnp.concatenate(hots, axis=1),
        grad_ref[pl.ds(k, SPREAD)].reshape(SPREAD * count, width),
    )

    @pl.when(step == 0)
    def start():
        total[...] = part

    @pl.when(step > 0)
    def go_on():
        total[...] += part

    @pl.when(step == pl.num_programs(0) - 1)
    def finish():
        result = split_back(total[...], weight_ref[...])
        if base:
            result = result + base[0][first : first + rows, :]
        out_ref[...] = result.astype(out_ref.dtype)


def spread(index, grad, weight, first, rows, dtype, *base):
    degree, count, width = grad.shape
    resident = pl.BlockSpec(memory_space=pltpu.VMEM)
    return pl.pallas_call(
        functools.partial(spread_kernel, first),
        grid=(degree // SPREAD,),
        in_specs=[resident] * (3 + len(base)),
        out_specs=resident,
        out_shape=pltpu.VMEM((rows, width), dtype),
        scratch_shapes=[pltpu.VMEM((rows, width), F32)],
        compiler_params=params(),
        cost_estimate=cost(2 * rows * grad.size, 2 * grad.size),
        name="spread_rows",
    )(index, grad, weight, *base)


def edge_kernel(grad_ref, weight_ref, out_ref, turned):
    slots, rows, width = out_ref.shape

    @pl.when(pl.program_id(0) == 0)
    def turn():
        turned[...] = weight_ref[...].T

    grad = grad_ref[pl.ds(pl.program_id(0) * slots, slots)].reshape(slots * rows, width)
    out_ref[...] = dot(grad, turned[...]).astype(BF16).reshape(slots, rows, width)


def edge_grads(grad, weight):
    degree, count, width = grad.shape
    resident = pl.BlockSpec(memory_space=pltpu.VMEM)
    return pl.pallas_call(
        edge_kernel,
        grid=(degree // EDGE,),
        in_specs=[resident, resident],
        out_specs=pl.BlockSpec((EDGE, count, width), lambda i: (i, 0, 0)),
        out_shape=jax.ShapeDtypeStruct(grad.shape, BF16),
        scratch_shapes=[pltpu.VMEM((width, width), BF16)],
        compiler_params=params(),
        cost_estimate=cost(2 * grad.size * width, 4 * grad.size),
        name="edge_grads",
    )(grad, weight)


def split_kernel(keep_ref, came_ref, own_ref, *away_refs):
    part = own_ref.shape[0]
    for p, out_ref in enumerate((own_ref,) + away_refs):
        here = slice(p * part, (p + 1) * part)
        total = keep_ref[here, :] + came_ref[here, :].astype(F32)
        out_ref[...] = total.astype(out_ref.dtype)


def add_and_split(keep, came):
    part, width = keep.shape[0] // 4, keep.shape[1]
    return pl.pallas_call(
        split_kernel,
        out_shape=(pltpu.VMEM((part, width), F32),) + (pltpu.VMEM((part, width), BF16),) * 3,
        compiler_params=params(),
        cost_estimate=cost(keep.size, 8 * keep.size),
        name="add_and_split",
    )(keep, came)


def sum_kernel(own_ref, *refs):
    *came, out_ref = refs
    values = [own_ref[...].astype(F32)] + [r[...].astype(F32) for r in came]
    while len(values) > 1:
        values = [a + b for a, b in zip(values[::2], values[1::2])]
    out_ref[...] = values[0].astype(BF16)


def sum_parts(own, came):
    return pl.pallas_call(
        sum_kernel,
        out_shape=pltpu.VMEM(own.shape, BF16),
        compiler_params=params(),
        cost_estimate=cost(own.size * len(came), 8 * own.size),
        name="sum_parts",
    )(own, *came)


def join_kernel(*refs):
    *pieces, out_ref = refs
    at = 0
    for piece in pieces:
        out_ref[at : at + piece.shape[0], :] = piece[...]
        at += piece.shape[0]


def joined_parts(pieces):
    rows = sum(piece.shape[0] for piece in pieces)
    return pl.pallas_call(
        join_kernel,
        out_shape=pltpu.VMEM((rows, pieces[0].shape[1]), BF16),
        compiler_params=params(),
        name="join_parts",
    )(*pieces)


def finish_kernel(part_rows, place_ref, *refs):
    pieces, (lists_ref, low_ref, high_ref, next_ref, prev_ref) = refs[:5], refs[5:10]
    nodes_ref, outs, full = refs[10], refs[11:-1], refs[-1]
    low = low_ref.shape[0]
    for first, part_ref in ((0, low_ref), (low, high_ref)):
        count = part_ref.shape[0]
        hots = [hot_rows(lists_ref[side : side + 1, :], first, count) for side in range(2)]
        returned = jnp.concatenate([next_ref[...], prev_ref[...]], axis=0)
        nodes_ref[first : first + count, :] = part_ref[...] + dot(
            jnp.concatenate(hots, axis=1), returned
        )
    place = place_ref[0]
    p = 0
    for piece in pieces:
        for at in range(0, piece.shape[0], part_rows):
            start = pl.multiple_of((place ^ p) * part_rows, 16)
            full[pl.ds(start, part_rows), :] = piece[at : at + part_rows, :].astype(F32)
            p += 1
    at = 0
    for out_ref in outs:
        count = out_ref.shape[0]
        out_ref[...] = full[at : at + count, :]
        at += count


def finish(place, pieces, lists, low, high, ret_next, ret_prev, row_counts):
    part_rows, width = pieces[0].shape
    rows = low.shape[0] + high.shape[0]
    held = [*pieces, lists, low, high, ret_next, ret_prev]
    return pl.pallas_call(
        functools.partial(finish_kernel, part_rows),
        in_specs=[pl.BlockSpec(memory_space=pltpu.SMEM)]
        + [pl.BlockSpec(memory_space=pltpu.VMEM)] * len(held),
        out_shape=(jax.ShapeDtypeStruct((rows, width), F32),)
        + tuple(jax.ShapeDtypeStruct((n, width), F32) for n in row_counts),
        scratch_shapes=[pltpu.VMEM((8 * part_rows, width), F32)],
        compiler_params=params(),
        cost_estimate=cost(4 * rows * ret_next.size, 8 * rows * width),
        name="finish",
    )(place, *held)


def traded(value, mask):
    count = lax.axis_size("face") * lax.axis_size("sub")
    return lax.ppermute(value, BOTH, [(i, i ^ mask) for i in range(count)])


def tied(*values):
    return lax.optimization_barrier(values)


def passed_along(value, steps):
    count = lax.axis_size("face")
    pairs = [(source, (source + steps) % count) for source in range(count)]
    return lax.ppermute(value, "face", pairs)


def body(
    nodes,
    edges,
    neighbours,
    valid,
    send_lists,
    edge_first,
    edge_first_bias,
    edge_second,
    edge_second_bias,
    edge_gain,
    edge_shift,
    node_first,
    node_first_bias,
    node_second,
    node_second_bias,
    node_gain,
    node_shift,
    cotangent,
):
    rows, width = nodes.shape
    lists = send_lists[0]
    halo_rows = lists.shape[1]
    index = neighbours.T
    flags = valid.T
    edge_rows = jnp.transpose(edges, (1, 0, 2))
    vec = jnp.stack(
        [
            edge_first_bias,
            edge_second_bias,
            edge_gain,
            edge_shift,
            node_first_bias,
            node_second_bias,
            node_gain,
            node_shift,
        ]
    ).astype(F32)
    subs = lax.axis_size("sub")
    me = lax.axis_index("face") * subs + lax.axis_index("sub")
    devices = lax.axis_size("face") * subs
    masks = [1 << b for b in range(devices.bit_length() - 1)]
    masks = [subs] + [m for m in masks if m != subs]
    halving, doubling = masks[:3], masks[3:]
    place = jnp.int32(0)
    for mask in halving:
        place = place * 2 + jnp.where((me & mask) != 0, 1, 0)
    place = place.astype(jnp.int32).reshape(1)

    to_next, to_prev, nodes_held, index_held = pick(lists, nodes, index)
    from_prev = passed_along(to_next, 1)
    from_next = passed_along(to_prev, -1)
    own = own_senders(index_held, nodes_held)
    halo = jnp.concatenate([from_prev, from_next], axis=0)
    weights = [in_vmem(a) for a in (edge_first, edge_second, node_first, node_second)]
    mixed, grad_nodes, grad_a, away, keep = main(
        place,
        index_held,
        in_vmem(flags),
        edge_rows,
        own,
        nodes_held,
        in_vmem(halo),
        in_vmem(cotangent),
        in_vmem(vec),
        *weights,
        1 << len(halving),
    )
    send_weight = edge_first[width : 2 * width]
    edge_weight = edge_first[2 * width :]
    half = rows // 2
    core, outer, inner = halving
    plane = (inner, outer, inner ^ outer)

    came = traded(away, core)
    part, *away = add_and_split(keep, came)
    came = [traded(a, mask) for a, mask in zip(away, plane)]
    grad_a, part = tied(grad_a, part)
    back = spread(index_held, grad_a, send_weight, rows, 2 * halo_rows, BF16)
    came, back = tied(came, back)
    part = sum_parts(part, came)
    ret_next = passed_along(back[:halo_rows], -1)
    ret_prev = passed_along(back[halo_rows:], 1)
    while doubling:
        first, *doubling = doubling
        group = [first]
        if doubling:
            second, *doubling = doubling
            group = [first, second, first ^ second]
        came = [traded(part, mask) for mask in group]
        if not doubling:
            grad_a, part = tied(grad_a, part)
            low = spread(index_held, grad_a, send_weight, 0, half, F32, grad_nodes)
            grad_edges = edge_grads(grad_a, edge_weight)
            came, low, grad_edges = tied(came, low, grad_edges)
        part = sum_parts(part, came)
    came = [traded(part, mask) for mask in plane]
    grad_a, part, ret_next, ret_prev = tied(grad_a, part, ret_next, ret_prev)
    high = spread(index_held, grad_a, send_weight, half, half, F32, grad_nodes)
    came, high = tied(came, high)
    pieces = [part] + came
    pieces.append(traded(joined_parts(pieces), core))
    counts = (edge_first.shape[0], width, node_first.shape[0], width) + (1,) * 8
    grad_nodes, *sums = finish(place, pieces, lists, low, high, ret_next, ret_prev, counts)
    vectors = [v.reshape(width) for v in sums[4:]]
    return (
        mixed,
        grad_nodes,
        jnp.transpose(grad_edges, (1, 0, 2)),
        sums[0],
        vectors[0],
        sums[1],
        vectors[1],
        vectors[2],
        vectors[3],
        sums[2],
        vectors[4],
        sums[3],
        vectors[5],
        vectors[6],
        vectors[7],
    )


def solution(mesh):
    shared = P(("face", "sub"), None)
    split3 = P(("face", "sub"), None, None)
    return jax.shard_map(
        body,
        mesh=mesh,
        in_specs=(shared, split3, shared, shared, split3) + (P(),) * 12 + (shared,),
        out_specs=(shared, shared, split3) + (P(),) * 12,
        check_vma=False,
    )
```

```python
import functools

import jax
import jax.numpy as jnp
from jax import lax
from jax.experimental import pallas as pl
from jax.experimental.pallas import tpu as pltpu
from jax.sharding import PartitionSpec as P

F32 = jnp.float32
BF16 = jnp.bfloat16
LANES = 128
BLOCK = 128
PARTS = 5
PARTS2 = 5
CHUNK = 64
OWN = 3
SPREAD = 6
EDGE = 3
BOTH = ("face", "sub")
MIB = 1024 * 1024
VMEM_LIMIT = 30 * MIB


def params(limit=VMEM_LIMIT):
    return pltpu.CompilerParams(vmem_limit_bytes=limit)


def cost(flops, moved):
    return pl.CostEstimate(flops=int(flops), bytes_accessed=int(moved), transcendentals=0)


def dot(left, right):
    return jnp.dot(left, right, preferred_element_type=F32)


def dot_rows(left, right):
    return lax.dot_general(left, right, (((0,), (0,)), ((), ())), preferred_element_type=F32)


def dot_back(left, right):
    return lax.dot_general(left, right, (((1,), (1,)), ((), ())), preferred_element_type=F32)


def down(row):
    return jnp.broadcast_to(row, (LANES, LANES)).T


def hot_lanes(index, first, count):
    lane = lax.broadcasted_iota(jnp.int32, (1, LANES), 1)
    index = index.astype(jnp.int16)
    one, zero = BF16(1.0), BF16(0.0)
    tiles = [
        jnp.where(index == (lane + (first + t * LANES)).astype(jnp.int16), one, zero)
        for t in range(count // LANES)
    ]
    return jnp.concatenate(tiles, axis=1)


def hot_rows(index, first, count):
    row = lax.broadcasted_iota(jnp.int32, (count, 1), 0) + first
    return jnp.where(row == index, 1.0, 0.0).astype(BF16)


def row_mean(values):
    return jnp.mean(values, axis=-1, keepdims=True)


def col_sum(values):
    return jnp.sum(values, axis=0, keepdims=True)


def gate(halves):
    twice = 1.0 + jnp.tanh(halves)
    act = halves * twice
    return act, twice + act * (2.0 - twice)


def norm(values):
    centre = values - row_mean(values)
    scale = lax.rsqrt(row_mean(centre * centre) + 1e-05)
    return centre * scale, scale


def pick_kernel(
    lists_hbm, nodes_hbm, index_hbm, next_ref, prev_ref, nodes_ref, index_ref, lists_ref, sems
):
    pairs = ((lists_hbm, lists_ref), (nodes_hbm, nodes_ref), (index_hbm, index_ref))
    copies = [pltpu.make_async_copy(a, b, sems.at[i]) for i, (a, b) in enumerate(pairs)]
    for copy in copies:
        copy.start()
    for copy in copies:
        copy.wait()
    rows = nodes_ref.shape[0]
    halo = lists_ref.shape[1]
    for side, out_ref in ((0, next_ref), (1, prev_ref)):
        for at in range(0, halo, LANES):
            picked = down(lists_ref[side : side + 1, at : at + LANES])
            out_ref[at : at + LANES, :] = dot(
                hot_lanes(picked, 0, rows), nodes_ref[...]
            ).astype(BF16)


def in_hbm(array):
    return pltpu.with_memory_space_constraint(array, pltpu.HBM)


def pick(lists, nodes, index):
    halo, width = lists.shape[1], nodes.shape[1]
    out = pltpu.VMEM((halo, width), BF16)
    return pl.pallas_call(
        pick_kernel,
        in_specs=[pl.BlockSpec(memory_space=pltpu.HBM)] * 3,
        out_specs=[pl.BlockSpec(memory_space=pltpu.VMEM)] * 4,
        out_shape=(out, out, pltpu.VMEM(nodes.shape, BF16), pltpu.VMEM(index.shape, jnp.int32)),
        scratch_shapes=[pltpu.VMEM(lists.shape, jnp.int32), pltpu.SemaphoreType.DMA((3,))],
        compiler_params=params(),
        cost_estimate=cost(4 * halo * nodes.size, 2 * nodes.size),
        name="pick_rows",
    )(in_hbm(lists), in_hbm(nodes), in_hbm(index))


def in_vmem(array):
    return pltpu.with_memory_space_constraint(array, pltpu.VMEM)


def own_kernel(index_ref, nodes_ref, out_ref):
    rows = nodes_ref.shape[0]
    slots = out_ref.shape[0]
    for j in range(slots):
        row = index_ref[pl.ds(pl.program_id(0) * slots + j, 1), :]
        column = jnp.concatenate(
            [down(row[:, at : at + LANES]) for at in range(0, rows, LANES)], axis=0
        )
        out_ref[j] = dot(hot_lanes(column, 0, rows), nodes_ref[...]).astype(BF16)


def own_senders(index, nodes):
    degree, rows = index.shape
    width = nodes.shape[1]
    return pl.pallas_call(
        own_kernel,
        grid=(degree // OWN,),
        in_specs=[pl.BlockSpec(memory_space=pltpu.VMEM)] * 2,
        out_specs=pl.BlockSpec((OWN, rows, width), lambda i: (i, 0, 0)),
        out_shape=pltpu.HBM((degree, rows, width), BF16),
        compiler_params=params(30 * MIB),
        cost_estimate=cost(2 * degree * rows * rows * width, 2 * degree * rows * width),
        name="own_senders",
    )(index, nodes)


def main_kernel(
    degree,
    part_rows,
    place_ref,
    edges_ref,
    own_ref,
    index_ref,
    valid_ref,
    nodes_ref,
    halo_ref,
    cot_ref,
    vec_ref,
    w_first_ref,
    w_second_ref,
    n_first_ref,
    n_second_ref,
    mixed_hbm,
    grad_nodes_ref,
    hat_ref,
    away_ref,
    keep_ref,
    snd_ref,
    act_scr,
    slope_scr,
    scale_scr,
    sum_scr,
    count_scr,
    up_scr,
    acc_scr,
    turned_scr,
    half_first,
    half_second,
    bias_scr,
    mixed_ref,
    mixed_sem,
    centred,
):
    step = pl.program_id(0)
    rows, width = nodes_ref.shape
    e_b1, e_b2, e_gain, e_shift, n_b1, n_b2, n_gain, n_shift = (
        vec_ref[i : i + 1, :] for i in range(8)
    )
    at_first, at_second = 0, 3 * width
    at_nfirst, at_nsecond, at_vec = 4 * width, 6 * width, 7 * width

    def wide(lanes):
        return jnp.concatenate([lanes] * (width // LANES), axis=1)

    @pl.when(step == 0)
    def begin():
        half_first[...] = (w_first_ref[...].astype(F32) * 0.5).astype(BF16)
        second = w_second_ref[...].astype(F32)
        half_second[...] = (second * 0.5).astype(BF16)
        centred[...] = (second - row_mean(second)).astype(BF16)
        sum_scr[...] = jnp.zeros(sum_scr.shape, F32)
        count_scr[...] = jnp.zeros(count_scr.shape, F32)
        bias_scr[...] = jnp.zeros(bias_scr.shape, F32)
        acc_scr[...] = jnp.zeros(acc_scr.shape, F32)
        turned_scr[...] = jnp.zeros(turned_scr.shape, F32)
        up_scr[...] = dot(nodes_ref[...], half_first[:width, :]) + 0.5 * e_b1

    @pl.when(step < degree)
    def forward():
        k = step
        joint = index_ref[pl.ds(k, 1), :] * 2 + valid_ref[pl.ds(k, 1), :]
        part = rows // PARTS
        centred_b2 = e_b2 - row_mean(e_b2)
        columns, entered = {}, {}

        def choose(p):
            column = jnp.concatenate(
                [down(joint[:, at : at + LANES]) for at in range(p * part, (p + 1) * part, LANES)],
                axis=0,
            )
            columns[p] = column
            return dot(hot_lanes(column >> 1, rows, halo_ref.shape[0]), halo_ref[...])

        def enter(p, picked):
            here = slice(p * part, (p + 1) * part)
            snd = picked.astype(BF16) + own_ref[0, here, :]
            snd_ref[k, here, :] = snd
            joined = jnp.concatenate([snd, edges_ref[0, here, :]], axis=1)
            return dot(joined, half_first[width:, :])

        def middle(p, pre):
            acts = []
            for at in range(0, part, CHUNK):
                here = slice(p * part + at, p * part + at + CHUNK)
                act, slope = gate(pre[at : at + CHUNK] + up_scr[here, :])
                act = act.astype(BF16)
                acts.append(act)
                act_scr[k, here, :] = act
                slope_scr[k, here, :] = slope.astype(BF16)
            return dot(jnp.concatenate(acts, axis=0), centred[...])

        def leave(p, second):
            for at in range(0, part, CHUNK):
                here = slice(p * part + at, p * part + at + CHUNK)
                live = (columns[p][at : at + CHUNK] & 1).astype(F32)
                centre = second[at : at + CHUNK] + centred_b2
                scale = lax.rsqrt(row_mean(centre * centre) + 1e-05) * live
                hat = centre * wide(scale)
                hat_ref[k, here, :] = hat.astype(BF16)
                scale_scr[k, here, :] = scale.astype(scale_scr.dtype)
                sum_scr[here, :] += hat
                count_scr[here, :] += live

        chosen, seconds = {}, {}
        for i in range(PARTS):
            chosen[i] = choose(i)
        for i in range(PARTS):
            entered[i] = enter(i, chosen.pop(i))
        for i in range(PARTS):
            seconds[i] = middle(i, entered.pop(i))
        for i in range(PARTS):
            leave(i, seconds.pop(i))

    @pl.when(step == degree)
    def node_stage():
        part = rows // PARTS
        parts = [slice(p * part, (p + 1) * part) for p in range(PARTS)]
        gathered, firsts, acts, slopes, seconds = [], [], [], [], []
        hats, grads_d, grads_c, backs = [], [], [], []
        for here in parts:
            counts = wide(count_scr[here, :])
            gathered.append((sum_scr[here, :] * e_gain + counts * e_shift).astype(BF16))
            joined = jnp.concatenate([nodes_ref[here, :], gathered[-1]], axis=1)
            firsts.append(dot(joined, n_first_ref[...]))
        for first in firsts:
            act, slope = gate(0.5 * (first + n_b1))
            acts.append(act.astype(BF16))
            slopes.append(0.5 * slope)
            seconds.append(dot(acts[-1], n_second_ref[...]))
        ups, hat_sums, up_sums, d_sums, c_sums = [], [], [], [], []
        for here, second in zip(parts, seconds):
            hat, scale = norm(second + n_b2)
            out = nodes_ref[here, :].astype(F32) + (hat * n_gain + n_shift)
            mixed_ref[here, :] = out.astype(BF16)
            up = cot_ref[here, :].astype(F32)
            hat_sums.append(col_sum(up * hat))
            up_sums.append(col_sum(up))
            scaled = up * n_gain
            grad = scale * (scaled - row_mean(scaled) - hat * row_mean(scaled * hat))
            d_sums.append(col_sum(grad))
            grads_d.append(grad.astype(BF16))
            backs.append(dot_back(grads_d[-1], n_second_ref[...]))
        for p in range(PARTS):
            grad = backs[p] * slopes[p]
            c_sums.append(col_sum(grad))
            grads_c.append(grad.astype(BF16))
        all_d, all_c = jnp.concatenate(grads_d, axis=0), jnp.concatenate(grads_c, axis=0)
        acc_scr[at_nsecond : at_nsecond + width, :] = dot_rows(
            jnp.concatenate(acts, axis=0), all_d
        )
        for p, here in enumerate(parts):
            gain_part = dot_back(grads_c[p], n_first_ref[width:, :])
            own_part = dot_back(grads_c[p], n_first_ref[:width, :])
            grad_nodes_ref[here, :] = cot_ref[here, :].astype(F32) + own_part
            sums, counts = sum_scr[here, :], wide(count_scr[here, :])
            acc_scr[at_vec + 2 : at_vec + 3, :] += col_sum(gain_part * sums)
            acc_scr[at_vec + 3 : at_vec + 4, :] += col_sum(gain_part * counts)
            scaled = gain_part * e_gain
            up_scr[here, :] = scaled - row_mean(scaled)
            sum_scr[here, :] = jnp.zeros((part, width), F32)
        acc_scr[at_nfirst : at_nfirst + width, :] = dot_rows(nodes_ref[...], all_c)
        acc_scr[at_nfirst + width : at_nfirst + 2 * width, :] = dot_rows(
            jnp.concatenate(gathered, axis=0), all_c
        )
        pltpu.make_async_copy(mixed_ref, mixed_hbm, mixed_sem).start()
        for row, values in ((4, c_sums), (5, d_sums), (6, hat_sums), (7, up_sums)):
            acc_scr[at_vec + row : at_vec + row + 1, :] = sum(values)

    def outer(k):
        all_a = hat_ref[k]
        turned_scr[:, :width] += dot_rows(all_a, snd_ref[k])
        turned_scr[:, width:] += dot_rows(all_a, edges_ref[0])

    def backward(k):
        part = rows // PARTS2
        grads, backs = [], []
        for p in range(PARTS2):
            out = []
            for at in range(p * part, (p + 1) * part, CHUNK):
                here = slice(at, at + CHUNK)
                hat = hat_ref[k, here, :].astype(F32)
                scale = wide(scale_scr[k, here, :].astype(F32))
                up = up_scr[here, :]
                grad = scale * (up - hat * row_mean(up * hat))
                bias_scr[...] += jnp.sum(grad.reshape(CHUNK // 8, 8, width), axis=0)
                out.append(grad.astype(BF16))
            grads.append(jnp.concatenate(out, axis=0))
            backs.append(dot_back(grads[-1], half_second[...]))
        acc_scr[at_second : at_second + width, :] += dot_rows(
            act_scr[k], jnp.concatenate(grads, axis=0)
        )
        for p in range(PARTS2):
            for at in range(0, part, CHUNK):
                here = slice(p * part + at, p * part + at + CHUNK)
                grad = backs[p][at : at + CHUNK] * slope_scr[k, here, :].astype(F32)
                sum_scr[here, :] += grad
                hat_ref[k, here, :] = grad.astype(BF16)

    @pl.when(step == degree)
    def first_back():
        backward(0)

    @pl.when((step > degree) & (step < 2 * degree))
    def go_back():
        outer(step - degree - 1)
        backward(step - degree)

    @pl.when(step == 2 * degree)
    def hand_over():
        outer(degree - 1)
        pltpu.make_async_copy(mixed_ref, mixed_hbm, mixed_sem).wait()
        acc_scr[at_vec + 1 : at_vec + 2, :] = col_sum(bias_scr[...])
        acc_scr[at_vec : at_vec + 1, :] = col_sum(sum_scr[...])
        received = sum_scr[...].astype(BF16)
        acc_scr[at_first : at_first + width, :] = dot_rows(nodes_ref[...], received)
        grad_nodes_ref[...] += dot_back(received, w_first_ref[:width, :])
        acc_scr[at_first + width : at_first + 3 * width, :] = turned_scr[...].T
        place = place_ref[0]
        half = keep_ref.shape[0] // part_rows
        for p in range(2 * half):
            start = pl.multiple_of((place ^ p) * part_rows, 16)
            piece = acc_scr[pl.ds(start, part_rows), :]
            if p < half:
                keep_ref[p * part_rows : (p + 1) * part_rows, :] = piece
            else:
                out = (p - half) * part_rows
                away_ref[out : out + part_rows, :] = piece.astype(BF16)


def main(place, index, valid, edges, own, nodes, halo, cot, vec, w1, w2, n1, n2, parts):
    degree, rows, width = edges.shape
    grad_rows = w1.shape[0] + w2.shape[0] + n1.shape[0] + n2.shape[0] + 8
    part_rows = -(-grad_rows // (16 * parts)) * 16
    total = part_rows * parts
    resident = pl.BlockSpec(memory_space=pltpu.VMEM)
    edge_spec = pl.BlockSpec((1, rows, width), lambda i, *_: (jnp.where(i > degree, i - degree - 1, jnp.minimum(i, degree - 1)), 0, 0))
    held = (index, valid, nodes, halo, cot, vec, w1, w2, n1, n2)
    own_spec = pl.BlockSpec(
        (1, rows, width), lambda i, *_: (jnp.minimum(i, degree - 1), 0, 0)
    )
    grid_spec = pltpu.PrefetchScalarGridSpec(
        num_scalar_prefetch=1,
        grid=(2 * degree + 1,),
        in_specs=[edge_spec, own_spec] + [resident] * len(held),
        out_specs=[pl.BlockSpec(memory_space=pltpu.HBM)] + [resident] * 4,
        scratch_shapes=[
            pltpu.VMEM((degree, rows, width), BF16),
            pltpu.VMEM((degree, rows, width), BF16),
            pltpu.VMEM((degree, rows, width), BF16),
            pltpu.VMEM((degree, rows, LANES), BF16),
            pltpu.VMEM((rows, width), F32),
            pltpu.VMEM((rows, LANES), F32),
            pltpu.VMEM((rows, width), F32),
            pltpu.VMEM((total, width), F32),
            pltpu.VMEM((width, 2 * width), F32),
            pltpu.VMEM(w1.shape, BF16),
            pltpu.VMEM(w2.shape, BF16),
            pltpu.VMEM((8, width), F32),
            pltpu.VMEM((rows, width), BF16),
            pltpu.SemaphoreType.DMA,
            pltpu.VMEM(w2.shape, BF16),
        ],
    )
    return pl.pallas_call(
        functools.partial(main_kernel, degree, part_rows),
        grid_spec=grid_spec,
        out_shape=(
            pltpu.HBM((rows, width), BF16),
            pltpu.VMEM((rows, width), F32),
            pltpu.VMEM((degree, rows, width), BF16),
            pltpu.VMEM((total // 2, width), BF16),
            pltpu.VMEM((total // 2, width), F32),
        ),
        compiler_params=params(46 * MIB),
        cost_estimate=cost(18 * degree * rows * width * width, 8 * edges.size),
        name="edges_and_nodes",
    )(place, edges, pltpu.with_memory_space_constraint(own, pltpu.HBM), *held)


def split_back(total, weight):
    high = total.astype(BF16)
    low = (total - high.astype(F32)).astype(BF16)
    return dot_back(high, weight) + dot_back(low, weight)


def spread_kernel(first, index_ref, grad_ref, weight_ref, *rest):
    *base, out_ref, total = rest
    degree, count, width = grad_ref.shape
    rows = total.shape[0]
    step = pl.program_id(0)
    k = step * SPREAD
    hots = [hot_rows(index_ref[pl.ds(k + j, 1), :], first, rows) for j in range(SPREAD)]
    part = dot(
        jnp.concatenate(hots, axis=1),
        grad_ref[pl.ds(k, SPREAD)].reshape(SPREAD * count, width),
    )

    @pl.when(step == 0)
    def start():
        total[...] = part

    @pl.when(step > 0)
    def go_on():
        total[...] += part

    @pl.when(step == pl.num_programs(0) - 1)
    def finish():
        result = split_back(total[...], weight_ref[...])
        if base:
            result = result + base[0][first : first + rows, :]
        out_ref[...] = result.astype(out_ref.dtype)


def spread(index, grad, weight, first, rows, dtype, *base):
    degree, count, width = grad.shape
    resident = pl.BlockSpec(memory_space=pltpu.VMEM)
    return pl.pallas_call(
        functools.partial(spread_kernel, first),
        grid=(degree // SPREAD,),
        in_specs=[resident] * (3 + len(base)),
        out_specs=resident,
        out_shape=pltpu.VMEM((rows, width), dtype),
        scratch_shapes=[pltpu.VMEM((rows, width), F32)],
        compiler_params=params(),
        cost_estimate=cost(2 * rows * grad.size, 2 * grad.size),
        name="spread_rows",
    )(index, grad, weight, *base)


def edge_kernel(grad_ref, weight_ref, out_ref, turned):
    slots, rows, width = out_ref.shape

    @pl.when(pl.program_id(0) == 0)
    def turn():
        turned[...] = weight_ref[...].T

    grad = grad_ref[pl.ds(pl.program_id(0) * slots, slots)].reshape(slots * rows, width)
    out_ref[...] = dot(grad, turned[...]).astype(BF16).reshape(slots, rows, width)


def edge_grads(grad, weight):
    degree, count, width = grad.shape
    resident = pl.BlockSpec(memory_space=pltpu.VMEM)
    return pl.pallas_call(
        edge_kernel,
        grid=(degree // EDGE,),
        in_specs=[resident, resident],
        out_specs=pl.BlockSpec((EDGE, count, width), lambda i: (i, 0, 0)),
        out_shape=jax.ShapeDtypeStruct(grad.shape, BF16),
        scratch_shapes=[pltpu.VMEM((width, width), BF16)],
        compiler_params=params(),
        cost_estimate=cost(2 * grad.size * width, 4 * grad.size),
        name="edge_grads",
    )(grad, weight)


def split_kernel(keep_ref, came_ref, own_ref, *away_refs):
    part = own_ref.shape[0]
    for p, out_ref in enumerate((own_ref,) + away_refs):
        here = slice(p * part, (p + 1) * part)
        total = keep_ref[here, :] + came_ref[here, :].astype(F32)
        out_ref[...] = total.astype(out_ref.dtype)


def add_and_split(keep, came):
    part, width = keep.shape[0] // 4, keep.shape[1]
    return pl.pallas_call(
        split_kernel,
        out_shape=(pltpu.VMEM((part, width), F32),) + (pltpu.VMEM((part, width), BF16),) * 3,
        compiler_params=params(),
        cost_estimate=cost(keep.size, 8 * keep.size),
        name="add_and_split",
    )(keep, came)


def sum_kernel(own_ref, *refs):
    *came, out_ref = refs
    values = [own_ref[...].astype(F32)] + [r[...].astype(F32) for r in came]
    while len(values) > 1:
        values = [a + b for a, b in zip(values[::2], values[1::2])]
    out_ref[...] = values[0].astype(BF16)


def sum_parts(own, came):
    return pl.pallas_call(
        sum_kernel,
        out_shape=pltpu.VMEM(own.shape, BF16),
        compiler_params=params(),
        cost_estimate=cost(own.size * len(came), 8 * own.size),
        name="sum_parts",
    )(own, *came)


def join_kernel(*refs):
    *pieces, out_ref = refs
    at = 0
    for piece in pieces:
        out_ref[at : at + piece.shape[0], :] = piece[...]
        at += piece.shape[0]


def joined_parts(pieces):
    rows = sum(piece.shape[0] for piece in pieces)
    return pl.pallas_call(
        join_kernel,
        out_shape=pltpu.VMEM((rows, pieces[0].shape[1]), BF16),
        compiler_params=params(),
        name="join_parts",
    )(*pieces)


def returned_kernel(lists_ref, low_ref, high_ref, next_ref, prev_ref, nodes_ref):
    low = low_ref.shape[0]
    for first, part_ref in ((0, low_ref), (low, high_ref)):
        count = part_ref.shape[0]
        hots = [hot_rows(lists_ref[side : side + 1, :], first, count) for side in range(2)]
        returned = jnp.concatenate([next_ref[...], prev_ref[...]], axis=0)
        nodes_ref[first : first + count, :] = part_ref[...] + dot(
            jnp.concatenate(hots, axis=1), returned
        )


def returned_rows(lists, low, high, ret_next, ret_prev):
    rows, width = low.shape[0] + high.shape[0], low.shape[1]
    return pl.pallas_call(
        returned_kernel,
        out_shape=jax.ShapeDtypeStruct((rows, width), F32),
        compiler_params=params(),
        cost_estimate=cost(4 * rows * ret_next.size, 8 * rows * width),
        name="returned_rows",
    )(lists, low, high, ret_next, ret_prev)


def unpack_kernel(part_rows, place_ref, *refs):
    pieces, outs, full = refs[:5], refs[5:-1], refs[-1]
    place = place_ref[0]
    p = 0
    for piece in pieces:
        for at in range(0, piece.shape[0], part_rows):
            start = pl.multiple_of((place ^ p) * part_rows, 16)
            full[pl.ds(start, part_rows), :] = piece[at : at + part_rows, :].astype(F32)
            p += 1
    at = 0
    for out_ref in outs:
        count = out_ref.shape[0]
        out_ref[...] = full[at : at + count, :]
        at += count


def unpack(place, pieces, row_counts):
    part_rows, width = pieces[0].shape
    return pl.pallas_call(
        functools.partial(unpack_kernel, part_rows),
        in_specs=[pl.BlockSpec(memory_space=pltpu.SMEM)]
        + [pl.BlockSpec(memory_space=pltpu.VMEM)] * len(pieces),
        out_shape=tuple(jax.ShapeDtypeStruct((n, width), F32) for n in row_counts),
        scratch_shapes=[pltpu.VMEM((8 * part_rows, width), F32)],
        compiler_params=params(),
        name="unpack_sums",
    )(place, *pieces)


def traded(value, mask):
    count = lax.axis_size("face") * lax.axis_size("sub")
    return lax.ppermute(value, BOTH, [(i, i ^ mask) for i in range(count)])


def tied(*values):
    return lax.optimization_barrier(values)


def passed_along(value, steps):
    count = lax.axis_size("face")
    pairs = [(source, (source + steps) % count) for source in range(count)]
    return lax.ppermute(value, "face", pairs)


def body(
    nodes,
    edges,
    neighbours,
    valid,
    send_lists,
    edge_first,
    edge_first_bias,
    edge_second,
    edge_second_bias,
    edge_gain,
    edge_shift,
    node_first,
    node_first_bias,
    node_second,
    node_second_bias,
    node_gain,
    node_shift,
    cotangent,
):
    rows, width = nodes.shape
    lists = send_lists[0]
    halo_rows = lists.shape[1]
    index = neighbours.T
    flags = valid.T
    edge_rows = jnp.transpose(edges, (1, 0, 2))
    vec = jnp.stack(
        [
            edge_first_bias,
            edge_second_bias,
            edge_gain,
            edge_shift,
            node_first_bias,
            node_second_bias,
            node_gain,
            node_shift,
        ]
    ).astype(F32)
    subs = lax.axis_size("sub")
    me = lax.axis_index("face") * subs + lax.axis_index("sub")
    devices = lax.axis_size("face") * subs
    masks = [1 << b for b in range(devices.bit_length() - 1)]
    masks = [subs] + [m for m in masks if m != subs]
    halving, doubling = masks[:3], masks[3:]
    place = jnp.int32(0)
    for mask in halving:
        place = place * 2 + jnp.where((me & mask) != 0, 1, 0)
    place = place.astype(jnp.int32).reshape(1)

    to_next, to_prev, nodes_held, index_held = pick(lists, nodes, index)
    from_prev = passed_along(to_next, 1)
    from_next = passed_along(to_prev, -1)
    own = own_senders(index_held, nodes_held)
    halo = jnp.concatenate([from_prev, from_next], axis=0)
    weights = [in_vmem(a) for a in (edge_first, edge_second, node_first, node_second)]
    mixed, grad_nodes, grad_a, away, keep = main(
        place,
        index_held,
        in_vmem(flags),
        edge_rows,
        own,
        nodes_held,
        in_vmem(halo),
        in_vmem(cotangent),
        in_vmem(vec),
        *weights,
        1 << len(halving),
    )
    send_weight = edge_first[width : 2 * width]
    edge_weight = edge_first[2 * width :]
    half = rows // 2
    core, outer, inner = halving
    plane = (inner, outer, inner ^ outer)

    came = traded(away, core)
    part, *away = add_and_split(keep, came)
    came = [traded(a, mask) for a, mask in zip(away, plane)]
    grad_a, part = tied(grad_a, part)
    back = spread(index_held, grad_a, send_weight, rows, 2 * halo_rows, BF16)
    came, back = tied(came, back)
    part = sum_parts(part, came)
    ret_next = passed_along(back[:halo_rows], -1)
    ret_prev = passed_along(back[halo_rows:], 1)
    while doubling:
        first, *doubling = doubling
        group = [first]
        if doubling:
            second, *doubling = doubling
            group = [first, second, first ^ second]
        came = [traded(part, mask) for mask in group]
        if not doubling:
            grad_a, part = tied(grad_a, part)
            low = spread(index_held, grad_a, send_weight, 0, half, F32, grad_nodes)
            grad_edges = edge_grads(grad_a, edge_weight)
            came, low, grad_edges = tied(came, low, grad_edges)
        part = sum_parts(part, came)
    came = [traded(part, mask) for mask in plane]
    grad_a, part, ret_next, ret_prev = tied(grad_a, part, ret_next, ret_prev)
    high = spread(index_held, grad_a, send_weight, half, half, F32, grad_nodes)
    came, high = tied(came, high)
    pieces = [part] + came
    came = traded(joined_parts(pieces), core)
    grad_nodes = returned_rows(lists, low, high, ret_next, ret_prev)
    came, grad_nodes = tied(came, grad_nodes)
    pieces.append(came)
    counts = (edge_first.shape[0], width, node_first.shape[0], width) + (1,) * 8
    sums = unpack(place, pieces, counts)
    vectors = [v.reshape(width) for v in sums[4:]]
    return (
        mixed,
        grad_nodes,
        jnp.transpose(grad_edges, (1, 0, 2)),
        sums[0],
        vectors[0],
        sums[1],
        vectors[1],
        vectors[2],
        vectors[3],
        sums[2],
        vectors[4],
        sums[3],
        vectors[5],
        vectors[6],
        vectors[7],
    )


def solution(mesh):
    shared = P(("face", "sub"), None)
    split3 = P(("face", "sub"), None, None)
    return jax.shard_map(
        body,
        mesh=mesh,
        in_specs=(shared, split3, shared, shared, split3) + (P(),) * 12 + (shared,),
        out_specs=(shared, shared, split3) + (P(),) * 12,
        check_vma=False,
    )
```

```python
import functools

import jax
import jax.numpy as jnp
from jax import lax
from jax.experimental import pallas as pl
from jax.experimental.pallas import tpu as pltpu
from jax.sharding import PartitionSpec as P

F32 = jnp.float32
BF16 = jnp.bfloat16
LANES = 128
BLOCK = 128
PARTS = 5
PARTS2 = 5
CHUNK = 64
OWN = 3
SPREAD = 6
EDGE = 3
BOTH = ("face", "sub")
MIB = 1024 * 1024
VMEM_LIMIT = 30 * MIB


def params(limit=VMEM_LIMIT):
    return pltpu.CompilerParams(vmem_limit_bytes=limit)


def cost(flops, moved):
    return pl.CostEstimate(flops=int(flops), bytes_accessed=int(moved), transcendentals=0)


def dot(left, right):
    return jnp.dot(left, right, preferred_element_type=F32)


def dot_rows(left, right):
    return lax.dot_general(left, right, (((0,), (0,)), ((), ())), preferred_element_type=F32)


def dot_back(left, right):
    return lax.dot_general(left, right, (((1,), (1,)), ((), ())), preferred_element_type=F32)


def down(row):
    return jnp.broadcast_to(row, (LANES, LANES)).T


def hot_lanes(index, first, count):
    lane = lax.broadcasted_iota(jnp.int32, (1, LANES), 1)
    index = index.astype(jnp.int16)
    one, zero = BF16(1.0), BF16(0.0)
    tiles = [
        jnp.where(index == (lane + (first + t * LANES)).astype(jnp.int16), one, zero)
        for t in range(count // LANES)
    ]
    return jnp.concatenate(tiles, axis=1)


def hot_rows(index, first, count):
    row = lax.broadcasted_iota(jnp.int32, (count, 1), 0) + first
    return jnp.where(row == index, 1.0, 0.0).astype(BF16)


def row_mean(values):
    return jnp.mean(values, axis=-1, keepdims=True)


def col_sum(values):
    return jnp.sum(values, axis=0, keepdims=True)


def gate(halves):
    twice = 1.0 + jnp.tanh(halves)
    act = halves * twice
    return act, twice + act * (2.0 - twice)


def norm(values):
    centre = values - row_mean(values)
    scale = lax.rsqrt(row_mean(centre * centre) + 1e-05)
    return centre * scale, scale


def pick_kernel(
    lists_hbm, nodes_hbm, index_hbm, next_ref, prev_ref, nodes_ref, index_ref, lists_ref, sems
):
    pairs = ((lists_hbm, lists_ref), (nodes_hbm, nodes_ref), (index_hbm, index_ref))
    copies = [pltpu.make_async_copy(a, b, sems.at[i]) for i, (a, b) in enumerate(pairs)]
    for copy in copies:
        copy.start()
    for copy in copies:
        copy.wait()
    rows = nodes_ref.shape[0]
    halo = lists_ref.shape[1]
    for side, out_ref in ((0, next_ref), (1, prev_ref)):
        for at in range(0, halo, LANES):
            picked = down(lists_ref[side : side + 1, at : at + LANES])
            out_ref[at : at + LANES, :] = dot(
                hot_lanes(picked, 0, rows), nodes_ref[...]
            ).astype(BF16)


def in_hbm(array):
    return pltpu.with_memory_space_constraint(array, pltpu.HBM)


def pick(lists, nodes, index):
    halo, width = lists.shape[1], nodes.shape[1]
    out = pltpu.VMEM((halo, width), BF16)
    return pl.pallas_call(
        pick_kernel,
        in_specs=[pl.BlockSpec(memory_space=pltpu.HBM)] * 3,
        out_specs=[pl.BlockSpec(memory_space=pltpu.VMEM)] * 4,
        out_shape=(out, out, pltpu.VMEM(nodes.shape, BF16), pltpu.VMEM(index.shape, jnp.int32)),
        scratch_shapes=[pltpu.VMEM(lists.shape, jnp.int32), pltpu.SemaphoreType.DMA((3,))],
        compiler_params=params(),
        cost_estimate=cost(4 * halo * nodes.size, 2 * nodes.size),
        name="pick_rows",
    )(in_hbm(lists), in_hbm(nodes), in_hbm(index))


def in_vmem(array):
    return pltpu.with_memory_space_constraint(array, pltpu.VMEM)


def own_kernel(index_ref, nodes_ref, out_ref):
    rows = nodes_ref.shape[0]
    slots = out_ref.shape[0]
    for j in range(slots):
        row = index_ref[pl.ds(pl.program_id(0) * slots + j, 1), :]
        column = jnp.concatenate(
            [down(row[:, at : at + LANES]) for at in range(0, rows, LANES)], axis=0
        )
        out_ref[j] = dot(hot_lanes(column, 0, rows), nodes_ref[...]).astype(BF16)


def own_senders(index, nodes):
    degree, rows = index.shape
    width = nodes.shape[1]
    return pl.pallas_call(
        own_kernel,
        grid=(degree // OWN,),
        in_specs=[pl.BlockSpec(memory_space=pltpu.VMEM)] * 2,
        out_specs=pl.BlockSpec((OWN, rows, width), lambda i: (i, 0, 0)),
        out_shape=pltpu.HBM((degree, rows, width), BF16),
        compiler_params=params(30 * MIB),
        cost_estimate=cost(2 * degree * rows * rows * width, 2 * degree * rows * width),
        name="own_senders",
    )(index, nodes)


def main_kernel(
    degree,
    part_rows,
    place_ref,
    edges_ref,
    own_ref,
    index_ref,
    valid_ref,
    nodes_ref,
    halo_ref,
    cot_ref,
    vec_ref,
    w_first_ref,
    w_second_ref,
    n_first_ref,
    n_second_ref,
    mixed_hbm,
    grad_nodes_ref,
    hat_ref,
    away_ref,
    keep_ref,
    snd_ref,
    act_scr,
    slope_scr,
    scale_scr,
    sum_scr,
    count_scr,
    up_scr,
    acc_scr,
    turned_scr,
    half_first,
    half_second,
    bias_scr,
    mixed_ref,
    mixed_sem,
    centred,
):
    step = pl.program_id(0)
    rows, width = nodes_ref.shape
    e_b1, e_b2, e_gain, e_shift, n_b1, n_b2, n_gain, n_shift = (
        vec_ref[i : i + 1, :] for i in range(8)
    )
    at_first, at_second = 0, 3 * width
    at_nfirst, at_nsecond, at_vec = 4 * width, 6 * width, 7 * width

    def wide(lanes):
        return jnp.concatenate([lanes] * (width // LANES), axis=1)

    @pl.when(step == 0)
    def begin():
        half_first[...] = (w_first_ref[...].astype(F32) * 0.5).astype(BF16)
        second = w_second_ref[...].astype(F32)
        half_second[...] = (second * 0.5).astype(BF16)
        centred[...] = (second - row_mean(second)).astype(BF16)
        sum_scr[...] = jnp.zeros(sum_scr.shape, F32)
        count_scr[...] = jnp.zeros(count_scr.shape, F32)
        bias_scr[...] = jnp.zeros(bias_scr.shape, F32)
        acc_scr[...] = jnp.zeros(acc_scr.shape, F32)
        turned_scr[...] = jnp.zeros(turned_scr.shape, F32)
        up_scr[...] = dot(nodes_ref[...], half_first[:width, :]) + 0.5 * e_b1

    @pl.when(step < degree)
    def forward():
        k = step
        joint = index_ref[pl.ds(k, 1), :] * 2 + valid_ref[pl.ds(k, 1), :]
        part = rows // PARTS
        centred_b2 = e_b2 - row_mean(e_b2)
        columns, entered = {}, {}

        def choose(p):
            column = jnp.concatenate(
                [down(joint[:, at : at + LANES]) for at in range(p * part, (p + 1) * part, LANES)],
                axis=0,
            )
            columns[p] = column
            return dot(hot_lanes(column >> 1, rows, halo_ref.shape[0]), halo_ref[...])

        def enter(p, picked):
            here = slice(p * part, (p + 1) * part)
            snd = picked.astype(BF16) + own_ref[0, here, :]
            snd_ref[k, here, :] = snd
            joined = jnp.concatenate([snd, edges_ref[0, here, :]], axis=1)
            return dot(joined, half_first[width:, :])

        def middle(p, pre):
            acts = []
            for at in range(0, part, CHUNK):
                here = slice(p * part + at, p * part + at + CHUNK)
                act, slope = gate(pre[at : at + CHUNK] + up_scr[here, :])
                act = act.astype(BF16)
                acts.append(act)
                act_scr[k, here, :] = act
                slope_scr[k, here, :] = slope.astype(BF16)
            return dot(jnp.concatenate(acts, axis=0), centred[...])

        def leave(p, second):
            for at in range(0, part, CHUNK):
                here = slice(p * part + at, p * part + at + CHUNK)
                live = (columns[p][at : at + CHUNK] & 1).astype(F32)
                centre = second[at : at + CHUNK] + centred_b2
                scale = lax.rsqrt(row_mean(centre * centre) + 1e-05) * live
                hat = centre * wide(scale)
                hat_ref[k, here, :] = hat.astype(BF16)
                scale_scr[k, here, :] = scale.astype(scale_scr.dtype)
                sum_scr[here, :] += hat
                count_scr[here, :] += live

        chosen, seconds = {}, {}
        for i in range(PARTS):
            chosen[i] = choose(i)
        for i in range(PARTS):
            entered[i] = enter(i, chosen.pop(i))
        for i in range(PARTS):
            seconds[i] = middle(i, entered.pop(i))
        for i in range(PARTS):
            leave(i, seconds.pop(i))

    @pl.when(step == degree)
    def node_stage():
        part = rows // PARTS
        parts = [slice(p * part, (p + 1) * part) for p in range(PARTS)]
        gathered, firsts, acts, slopes, seconds = [], [], [], [], []
        hats, grads_d, grads_c, backs = [], [], [], []
        for here in parts:
            counts = wide(count_scr[here, :])
            gathered.append((sum_scr[here, :] * e_gain + counts * e_shift).astype(BF16))
            joined = jnp.concatenate([nodes_ref[here, :], gathered[-1]], axis=1)
            firsts.append(dot(joined, n_first_ref[...]))
        for first in firsts:
            act, slope = gate(0.5 * (first + n_b1))
            acts.append(act.astype(BF16))
            slopes.append(0.5 * slope)
            seconds.append(dot(acts[-1], n_second_ref[...]))
        ups, hat_sums, up_sums, d_sums, c_sums = [], [], [], [], []
        for here, second in zip(parts, seconds):
            hat, scale = norm(second + n_b2)
            out = nodes_ref[here, :].astype(F32) + (hat * n_gain + n_shift)
            mixed_ref[here, :] = out.astype(BF16)
            up = cot_ref[here, :].astype(F32)
            hat_sums.append(col_sum(up * hat))
            up_sums.append(col_sum(up))
            scaled = up * n_gain
            grad = scale * (scaled - row_mean(scaled) - hat * row_mean(scaled * hat))
            d_sums.append(col_sum(grad))
            grads_d.append(grad.astype(BF16))
            backs.append(dot_back(grads_d[-1], n_second_ref[...]))
        for p in range(PARTS):
            grad = backs[p] * slopes[p]
            c_sums.append(col_sum(grad))
            grads_c.append(grad.astype(BF16))
        all_d, all_c = jnp.concatenate(grads_d, axis=0), jnp.concatenate(grads_c, axis=0)
        acc_scr[at_nsecond : at_nsecond + width, :] = dot_rows(
            jnp.concatenate(acts, axis=0), all_d
        )
        for p, here in enumerate(parts):
            gain_part = dot_back(grads_c[p], n_first_ref[width:, :])
            own_part = dot_back(grads_c[p], n_first_ref[:width, :])
            grad_nodes_ref[here, :] = cot_ref[here, :].astype(F32) + own_part
            sums, counts = sum_scr[here, :], wide(count_scr[here, :])
            acc_scr[at_vec + 2 : at_vec + 3, :] += col_sum(gain_part * sums)
            acc_scr[at_vec + 3 : at_vec + 4, :] += col_sum(gain_part * counts)
            scaled = gain_part * e_gain
            up_scr[here, :] = scaled - row_mean(scaled)
            sum_scr[here, :] = jnp.zeros((part, width), F32)
        acc_scr[at_nfirst : at_nfirst + width, :] = dot_rows(nodes_ref[...], all_c)
        acc_scr[at_nfirst + width : at_nfirst + 2 * width, :] = dot_rows(
            jnp.concatenate(gathered, axis=0), all_c
        )
        pltpu.make_async_copy(mixed_ref, mixed_hbm, mixed_sem).start()
        for row, values in ((4, c_sums), (5, d_sums), (6, hat_sums), (7, up_sums)):
            acc_scr[at_vec + row : at_vec + row + 1, :] = sum(values)

    def outer(k):
        all_a = hat_ref[k]
        turned_scr[:, :width] += dot_rows(all_a, snd_ref[k])
        turned_scr[:, width:] += dot_rows(all_a, edges_ref[0])

    def backward(k):
        part = rows // PARTS2
        grads, backs = [], []
        for p in range(PARTS2):
            out = []
            for at in range(p * part, (p + 1) * part, CHUNK):
                here = slice(at, at + CHUNK)
                hat = hat_ref[k, here, :].astype(F32)
                scale = wide(scale_scr[k, here, :].astype(F32))
                up = up_scr[here, :]
                grad = scale * (up - hat * row_mean(up * hat))
                bias_scr[...] += jnp.sum(grad.reshape(CHUNK // 8, 8, width), axis=0)
                out.append(grad.astype(BF16))
            grads.append(jnp.concatenate(out, axis=0))
            backs.append(dot_back(grads[-1], half_second[...]))
        acc_scr[at_second : at_second + width, :] += dot_rows(
            act_scr[k], jnp.concatenate(grads, axis=0)
        )
        for p in range(PARTS2):
            for at in range(0, part, CHUNK):
                here = slice(p * part + at, p * part + at + CHUNK)
                grad = backs[p][at : at + CHUNK] * slope_scr[k, here, :].astype(F32)
                sum_scr[here, :] += grad
                hat_ref[k, here, :] = grad.astype(BF16)

    @pl.when(step == degree)
    def first_back():
        backward(0)

    @pl.when((step > degree) & (step < 2 * degree))
    def go_back():
        outer(step - degree - 1)
        backward(step - degree)

    @pl.when(step == 2 * degree)
    def hand_over():
        outer(degree - 1)
        pltpu.make_async_copy(mixed_ref, mixed_hbm, mixed_sem).wait()
        acc_scr[at_vec + 1 : at_vec + 2, :] = col_sum(bias_scr[...])
        acc_scr[at_vec : at_vec + 1, :] = col_sum(sum_scr[...])
        received = sum_scr[...].astype(BF16)
        acc_scr[at_first : at_first + width, :] = dot_rows(nodes_ref[...], received)
        grad_nodes_ref[...] += dot_back(received, w_first_ref[:width, :])
        acc_scr[at_first + width : at_first + 3 * width, :] = turned_scr[...].T
        place = place_ref[0]
        half = keep_ref.shape[0] // part_rows
        for p in range(2 * half):
            start = pl.multiple_of((place ^ p) * part_rows, 16)
            piece = acc_scr[pl.ds(start, part_rows), :]
            if p < half:
                keep_ref[p * part_rows : (p + 1) * part_rows, :] = piece
            else:
                out = (p - half) * part_rows
                away_ref[out : out + part_rows, :] = piece.astype(BF16)


def main(place, index, valid, edges, own, nodes, halo, cot, vec, w1, w2, n1, n2, parts):
    degree, rows, width = edges.shape
    grad_rows = w1.shape[0] + w2.shape[0] + n1.shape[0] + n2.shape[0] + 8
    part_rows = -(-grad_rows // (16 * parts)) * 16
    total = part_rows * parts
    resident = pl.BlockSpec(memory_space=pltpu.VMEM)
    edge_spec = pl.BlockSpec((1, rows, width), lambda i, *_: (jnp.where(i > degree, i - degree - 1, jnp.minimum(i, degree - 1)), 0, 0))
    held = (index, valid, nodes, halo, cot, vec, w1, w2, n1, n2)
    own_spec = pl.BlockSpec(
        (1, rows, width), lambda i, *_: (jnp.minimum(i, degree - 1), 0, 0)
    )
    grid_spec = pltpu.PrefetchScalarGridSpec(
        num_scalar_prefetch=1,
        grid=(2 * degree + 1,),
        in_specs=[edge_spec, own_spec] + [resident] * len(held),
        out_specs=[pl.BlockSpec(memory_space=pltpu.HBM)] + [resident] * 4,
        scratch_shapes=[
            pltpu.VMEM((degree, rows, width), BF16),
            pltpu.VMEM((degree, rows, width), BF16),
            pltpu.VMEM((degree, rows, width), BF16),
            pltpu.VMEM((degree, rows, LANES), BF16),
            pltpu.VMEM((rows, width), F32),
            pltpu.VMEM((rows, LANES), F32),
            pltpu.VMEM((rows, width), F32),
            pltpu.VMEM((total, width), F32),
            pltpu.VMEM((width, 2 * width), F32),
            pltpu.VMEM(w1.shape, BF16),
            pltpu.VMEM(w2.shape, BF16),
            pltpu.VMEM((8, width), F32),
            pltpu.VMEM((rows, width), BF16),
            pltpu.SemaphoreType.DMA,
            pltpu.VMEM(w2.shape, BF16),
        ],
    )
    return pl.pallas_call(
        functools.partial(main_kernel, degree, part_rows),
        grid_spec=grid_spec,
        out_shape=(
            pltpu.HBM((rows, width), BF16),
            pltpu.VMEM((rows, width), F32),
            pltpu.VMEM((degree, rows, width), BF16),
            pltpu.VMEM((total // 2, width), BF16),
            pltpu.VMEM((total // 2, width), F32),
        ),
        compiler_params=params(46 * MIB),
        cost_estimate=cost(18 * degree * rows * width * width, 8 * edges.size),
        name="edges_and_nodes",
    )(place, edges, pltpu.with_memory_space_constraint(own, pltpu.HBM), *held)


def split_back(total, weight):
    high = total.astype(BF16)
    low = (total - high.astype(F32)).astype(BF16)
    return dot_back(high, weight) + dot_back(low, weight)


def spread_kernel(first, index_ref, grad_ref, weight_ref, *rest):
    *base, out_ref, total = rest
    degree, count, width = grad_ref.shape
    rows = total.shape[0]
    step = pl.program_id(0)
    k = step * SPREAD
    hots = [hot_rows(index_ref[pl.ds(k + j, 1), :], first, rows) for j in range(SPREAD)]
    part = dot(
        jnp.concatenate(hots, axis=1),
        grad_ref[pl.ds(k, SPREAD)].reshape(SPREAD * count, width),
    )

    @pl.when(step == 0)
    def start():
        total[...] = part

    @pl.when(step > 0)
    def go_on():
        total[...] += part

    @pl.when(step == pl.num_programs(0) - 1)
    def finish():
        result = split_back(total[...], weight_ref[...])
        if base:
            result = result + base[0][first : first + rows, :]
        out_ref[...] = result.astype(out_ref.dtype)


def spread(index, grad, weight, first, rows, dtype, *base):
    degree, count, width = grad.shape
    resident = pl.BlockSpec(memory_space=pltpu.VMEM)
    return pl.pallas_call(
        functools.partial(spread_kernel, first),
        grid=(degree // SPREAD,),
        in_specs=[resident] * (3 + len(base)),
        out_specs=resident,
        out_shape=pltpu.VMEM((rows, width), dtype),
        scratch_shapes=[pltpu.VMEM((rows, width), F32)],
        compiler_params=params(),
        cost_estimate=cost(2 * rows * grad.size, 2 * grad.size),
        name="spread_rows",
    )(index, grad, weight, *base)


def edge_kernel(grad_ref, weight_ref, out_ref, turned):
    slots, rows, width = out_ref.shape

    @pl.when(pl.program_id(0) == 0)
    def turn():
        turned[...] = weight_ref[...].T

    grad = grad_ref[pl.ds(pl.program_id(0) * slots, slots)].reshape(slots * rows, width)
    out_ref[...] = dot(grad, turned[...]).astype(BF16).reshape(slots, rows, width)


def edge_grads(grad, weight):
    degree, count, width = grad.shape
    resident = pl.BlockSpec(memory_space=pltpu.VMEM)
    return pl.pallas_call(
        edge_kernel,
        grid=(degree // EDGE,),
        in_specs=[resident, resident],
        out_specs=pl.BlockSpec((EDGE, count, width), lambda i: (i, 0, 0)),
        out_shape=jax.ShapeDtypeStruct(grad.shape, BF16),
        scratch_shapes=[pltpu.VMEM((width, width), BF16)],
        compiler_params=params(),
        cost_estimate=cost(2 * grad.size * width, 4 * grad.size),
        name="edge_grads",
    )(grad, weight)


def split_kernel(keep_ref, came_ref, own_ref, *away_refs):
    part = own_ref.shape[0]
    for p, out_ref in enumerate((own_ref,) + away_refs):
        here = slice(p * part, (p + 1) * part)
        total = keep_ref[here, :] + came_ref[here, :].astype(F32)
        out_ref[...] = total.astype(out_ref.dtype)


def add_and_split(keep, came):
    part, width = keep.shape[0] // 4, keep.shape[1]
    return pl.pallas_call(
        split_kernel,
        out_shape=(pltpu.VMEM((part, width), F32),) + (pltpu.VMEM((part, width), BF16),) * 3,
        compiler_params=params(),
        cost_estimate=cost(keep.size, 8 * keep.size),
        name="add_and_split",
    )(keep, came)


def sum_kernel(own_ref, *refs):
    *came, out_ref = refs
    values = [own_ref[...].astype(F32)] + [r[...].astype(F32) for r in came]
    while len(values) > 1:
        values = [a + b for a, b in zip(values[::2], values[1::2])]
    out_ref[...] = values[0].astype(BF16)


def sum_parts(own, came):
    return pl.pallas_call(
        sum_kernel,
        out_shape=pltpu.VMEM(own.shape, BF16),
        compiler_params=params(),
        cost_estimate=cost(own.size * len(came), 8 * own.size),
        name="sum_parts",
    )(own, *came)


def join_kernel(*refs):
    *pieces, out_ref = refs
    at = 0
    for piece in pieces:
        out_ref[at : at + piece.shape[0], :] = piece[...]
        at += piece.shape[0]


def joined_parts(pieces):
    rows = sum(piece.shape[0] for piece in pieces)
    return pl.pallas_call(
        join_kernel,
        out_shape=pltpu.VMEM((rows, pieces[0].shape[1]), BF16),
        compiler_params=params(),
        name="join_parts",
    )(*pieces)


def returned_kernel(lists_ref, low_ref, high_ref, next_ref, prev_ref, nodes_ref):
    low = low_ref.shape[0]
    for first, part_ref in ((0, low_ref), (low, high_ref)):
        count = part_ref.shape[0]
        hots = [hot_rows(lists_ref[side : side + 1, :], first, count) for side in range(2)]
        returned = jnp.concatenate([next_ref[...], prev_ref[...]], axis=0)
        nodes_ref[first : first + count, :] = part_ref[...] + dot(
            jnp.concatenate(hots, axis=1), returned
        )


def returned_rows(lists, low, high, ret_next, ret_prev):
    rows, width = low.shape[0] + high.shape[0], low.shape[1]
    return pl.pallas_call(
        returned_kernel,
        out_shape=jax.ShapeDtypeStruct((rows, width), F32),
        compiler_params=params(),
        cost_estimate=cost(4 * rows * ret_next.size, 8 * rows * width),
        name="returned_rows",
    )(lists, low, high, ret_next, ret_prev)


def unpack_kernel(part_rows, place_ref, *refs):
    pieces, outs, full = refs[:5], refs[5:-1], refs[-1]
    place = place_ref[0]
    p = 0
    for piece in pieces:
        for at in range(0, piece.shape[0], part_rows):
            start = pl.multiple_of((place ^ p) * part_rows, 16)
            full[pl.ds(start, part_rows), :] = piece[at : at + part_rows, :].astype(F32)
            p += 1
    at = 0
    for out_ref in outs:
        count = out_ref.shape[0]
        out_ref[...] = full[at : at + count, :]
        at += count


def unpack(place, pieces, row_counts):
    part_rows, width = pieces[0].shape
    return pl.pallas_call(
        functools.partial(unpack_kernel, part_rows),
        in_specs=[pl.BlockSpec(memory_space=pltpu.SMEM)]
        + [pl.BlockSpec(memory_space=pltpu.VMEM)] * len(pieces),
        out_shape=tuple(jax.ShapeDtypeStruct((n, width), F32) for n in row_counts),
        scratch_shapes=[pltpu.VMEM((8 * part_rows, width), F32)],
        compiler_params=params(),
        name="unpack_sums",
    )(place, *pieces)


def traded(value, mask):
    count = lax.axis_size("face") * lax.axis_size("sub")
    return lax.ppermute(value, BOTH, [(i, i ^ mask) for i in range(count)])


def tied(*values):
    return lax.optimization_barrier(values)


def passed_along(value, steps):
    count = lax.axis_size("face")
    pairs = [(source, (source + steps) % count) for source in range(count)]
    return lax.ppermute(value, "face", pairs)


def body(
    nodes,
    edges,
    neighbours,
    valid,
    send_lists,
    edge_first,
    edge_first_bias,
    edge_second,
    edge_second_bias,
    edge_gain,
    edge_shift,
    node_first,
    node_first_bias,
    node_second,
    node_second_bias,
    node_gain,
    node_shift,
    cotangent,
):
    rows, width = nodes.shape
    lists = send_lists[0]
    halo_rows = lists.shape[1]
    index = neighbours.T
    flags = valid.T
    edge_rows = jnp.transpose(edges, (1, 0, 2))
    vec = jnp.stack(
        [
            edge_first_bias,
            edge_second_bias,
            edge_gain,
            edge_shift,
            node_first_bias,
            node_second_bias,
            node_gain,
            node_shift,
        ]
    ).astype(F32)
    subs = lax.axis_size("sub")
    me = lax.axis_index("face") * subs + lax.axis_index("sub")
    devices = lax.axis_size("face") * subs
    masks = [1 << b for b in range(devices.bit_length() - 1)]
    masks = [subs] + [m for m in masks if m != subs]
    halving, doubling = masks[:3], masks[3:]
    place = jnp.int32(0)
    for mask in halving:
        place = place * 2 + jnp.where((me & mask) != 0, 1, 0)
    place = place.astype(jnp.int32).reshape(1)

    to_next, to_prev, nodes_held, index_held = pick(lists, nodes, index)
    from_prev = passed_along(to_next, 1)
    from_next = passed_along(to_prev, -1)
    own = own_senders(index_held, nodes_held)
    halo = jnp.concatenate([from_prev, from_next], axis=0)
    weights = [in_vmem(a) for a in (edge_first, edge_second, node_first, node_second)]
    mixed, grad_nodes, grad_a, away, keep = main(
        place,
        index_held,
        in_vmem(flags),
        edge_rows,
        own,
        nodes_held,
        in_vmem(halo),
        in_vmem(cotangent),
        in_vmem(vec),
        *weights,
        1 << len(halving),
    )
    send_weight = edge_first[width : 2 * width]
    edge_weight = edge_first[2 * width :]
    half = rows // 2
    core, outer, inner = halving
    plane = (inner, outer, inner ^ outer)

    came = traded(away, core)
    grad_edges = edge_grads(grad_a, edge_weight)
    came, grad_edges = tied(came, grad_edges)
    part, *away = add_and_split(keep, came)
    came = [traded(a, mask) for a, mask in zip(away, plane)]
    grad_a, part = tied(grad_a, part)
    back = spread(index_held, grad_a, send_weight, rows, 2 * halo_rows, BF16)
    came, back = tied(came, back)
    part = sum_parts(part, came)
    ret_next = passed_along(back[:halo_rows], -1)
    ret_prev = passed_along(back[halo_rows:], 1)
    while doubling:
        first, *doubling = doubling
        group = [first]
        if doubling:
            second, *doubling = doubling
            group = [first, second, first ^ second]
        came = [traded(part, mask) for mask in group]
        if not doubling:
            grad_a, part = tied(grad_a, part)
            low = spread(index_held, grad_a, send_weight, 0, half, F32, grad_nodes)
            came, low = tied(came, low)
        part = sum_parts(part, came)
    came = [traded(part, mask) for mask in plane]
    grad_a, part, ret_next, ret_prev = tied(grad_a, part, ret_next, ret_prev)
    high = spread(index_held, grad_a, send_weight, half, half, F32, grad_nodes)
    came, high = tied(came, high)
    pieces = [part] + came
    came = traded(joined_parts(pieces), core)
    grad_nodes = returned_rows(lists, low, high, ret_next, ret_prev)
    came, grad_nodes = tied(came, grad_nodes)
    pieces.append(came)
    counts = (edge_first.shape[0], width, node_first.shape[0], width) + (1,) * 8
    sums = unpack(place, pieces, counts)
    vectors = [v.reshape(width) for v in sums[4:]]
    return (
        mixed,
        grad_nodes,
        jnp.transpose(grad_edges, (1, 0, 2)),
        sums[0],
        vectors[0],
        sums[1],
        vectors[1],
        vectors[2],
        vectors[3],
        sums[2],
        vectors[4],
        sums[3],
        vectors[5],
        vectors[6],
        vectors[7],
    )


def solution(mesh):
    shared = P(("face", "sub"), None)
    split3 = P(("face", "sub"), None, None)
    return jax.shard_map(
        body,
        mesh=mesh,
        in_specs=(shared, split3, shared, shared, split3) + (P(),) * 12 + (shared,),
        out_specs=(shared, shared, split3) + (P(),) * 12,
        check_vma=False,
    )
```
